32 devices in a mesh: group: 2 (over y), ep: 8 (over z, core), dp: 2 (over x).
Axes of the slice: x: 2, y: 2, z: 4, core: 2. Of those that a mesh axis runs over, the one named last changes fastest.
Arguments:
- tokens: bfloat16 [256, 7168], P(('group', 'ep', 'dp')), parts along dimension 0, may hold values from -6 to 6
- expert_ids: int32 [256, 2], P(('group', 'ep', 'dp')), parts along dimension 0, may hold values from 0 to 7, all different within a row; in each aligned block of 8 rows (0 to 7, 8 to 15, ...) at most 3 rows name the same one
- gate_weights: float32 [256, 2], P(('group', 'ep', 'dp')), parts along dimension 0, may hold values from 0.5 to 2.5
- w_gate: bfloat16 [8, 7168, 2048], P('ep', None, 'dp'), may hold values from -0.0625 to 0.0625
- w_up: bfloat16 [8, 7168, 2048], P('ep', None, 'dp'), may hold values from -0.0625 to 0.0625
- w_down: bfloat16 [8, 2048, 7168], P('ep', 'dp'), may hold values from -0.125 to 0.125
- queries: bfloat16 [64, 128, 576], P(('group', 'ep', 'dp')), parts along dimension 0
- cache: bfloat16 [64, 512, 576], P(('group', 'ep', 'dp')), parts along dimension 0
- lengths: int32 [64], P(('group', 'ep', 'dp')), parts along dimension 0, may hold values from 1 to 512, 8192 in all
Outputs:
- moe_out: bfloat16 [256, 7168], P(('group', 'ep', 'dp')), parts along dimension 0
- attn_out: bfloat16 [64, 128, 512], P(('group', 'ep', 'dp')), parts along dimension 0
The draws below stay inside these ranges and needn't reach their ends.
There are 2 independent parts, one for each index of `group`. The reference program is written for one: setup_inputs(seed, part) draws one part's arguments, and reference() takes and returns one part's arrays. A program takes and returns all parts, laid end to end along the dimension named above; an argument that names none is the same for every part. Nothing has to cross between parts.
Inputs may be any that keep to these rules, and one draw needn't show every extreme that they name: `expert_ids`: in the rows of one device no expert is named by more than 3 routes, and some device reaches 3.
All inputs are finite; a program needn't handle non-finite values. No bound on the sum of `lengths` on one device may be relied on, other than what follows from the above.
Results may differ from the reference program's by a relative error of at most 0.009.
Values may be sent and summed in bfloat16 or wider, within the bound.
No kernel may reach another device: no remote copies, remote signals or barrier semaphores. Data moves between devices by JAX's collectives and lax.ppermute only.
A program may use at most 128 MiB of HBM per device.

```python
import math
import jax
import jax.numpy as jnp
import numpy as np
from jax import lax

D = 7168
HEADS = 128
LATENT = 512
ROPE = 64
FF = 2048
TOP = 2
TOK_DEV = 8
CACHE = 512
EXPERTS = 8
CAP = 3
TOKENS = 128
REQUESTS = 32
N_DP = 2


def cache_base(key):
    return jax.random.normal(key, (REQUESTS, CACHE, LATENT + ROPE), jnp.float32)


def draw_cache(key, part):
    base = cache_base(key)
    return base.astype(jnp.bfloat16)


def draw_queries(key, part):
    key = jax.random.fold_in(key, 11)
    values = jax.random.normal(key, (REQUESTS, HEADS, LATENT + ROPE), jnp.float32)
    return values.astype(jnp.bfloat16)


def levels(rng, extent, cuts, low, largest):
    loudness, own = 1.0, jax.random.fold_in(rng, 6)
    for position, blocks in cuts:
        steps = jnp.exp(jax.random.uniform(jax.random.fold_in(own, position), (blocks,), jnp.float32, low / len(cuts), largest / len(cuts)))
        loudness = loudness * jnp.repeat(steps, extent[position] // blocks).reshape([-1 if axis == position else 1 for axis in range(len(extent))])
    return loudness


def split_up(number_of, total, most, skew):
    weights = [(1 << 20) // math.isqrt(standing ** skew) + 1 for standing in range(2, number_of + 1)]
    spare, holding = total - most - (number_of - 1), [1] * (number_of - 1)
    while spare > 0:
        free = [i for i in range(number_of - 1) if holding[i] < most]
        pool, remaining = sum([weights[i] for i in free]), spare
        for i in free:
            addition = min(most - holding[i], max(1, remaining * weights[i] // pool), spare)
            holding[i] = holding[i] + addition
            spare = spare - addition
    return np.array([most] + holding)


def ragged_sizes(key, amount, total, bound, lean):
    if amount == 2:
        one = jax.random.randint(key, (), max(1, total - bound), min(bound, total - 1) + 1)
        return jnp.stack([one, total - one])
    tallies = jnp.asarray(split_up(amount, total, bound, lean), jnp.int32)
    twos = (amount - 1) // 2
    source_of, taker = tallies[1:1 + 2 * twos:2], tallies[2:2 + 2 * twos:2]
    room = jnp.minimum(source_of - 1, bound - taker)
    moved = jax.random.randint(jax.random.fold_in(key, 1), (twos,), 0, 1 << 20) % (room + 1)
    tallies = tallies.at[1:1 + 2 * twos:2].set(source_of - moved).at[2:2 + 2 * twos:2].set(taker + moved)
    return tallies[jax.random.permutation(jax.random.fold_in(key, 2), amount)]


def shared_out(stream_key, own, number, rows, amount, top, most, slope):
    sequence = jax.random.permutation(stream_key, amount)
    packed, usual = shares(amount, rows * top, most, slope, True), shares(amount, rows * top, most, slope, False)
    places = jnp.arange(amount)

    def named(sizes, turn):
        used = int((sizes > 0).sum())
        fixed = max(1, used // 4)
        shifted = fixed + (places - fixed + turn * (used - fixed)) % max(1, amount - fixed)
        return jnp.zeros((amount,), jnp.int32).at[sequence[jnp.where(places < fixed, places, shifted)]].set(jnp.asarray(sizes, jnp.int32))

    sizes = jnp.where(number % 4 == 0, named(packed, number // 4), named(usual, number - number // 4 - 1))
    mixed = jax.random.permutation(jax.random.fold_in(own, 3), amount)
    donor, receiver = mixed[0:amount // 2 * 2:2], mixed[1:amount // 2 * 2:2]
    slack = jnp.minimum(sizes[donor] - 1, most - sizes[receiver]) // 2
    slack = jnp.where((donor == sequence[0]) | (receiver == sequence[0]) | (sizes[receiver] == 0), 0, jnp.maximum(slack, 0))
    shifted = jax.random.randint(jax.random.fold_in(own, 4), (amount // 2,), 0, 1 << 20) % (slack + 1)
    sizes = sizes.at[donor].add(-shifted).at[receiver].add(shifted)
    members = jnp.searchsorted(jnp.cumsum(sizes), jnp.arange(rows * top), side="right").astype(jnp.int32)
    table = members.reshape(top, rows).T
    table = table[jax.random.permutation(jax.random.fold_in(own, 1), rows)]
    turn = jax.random.randint(jax.random.fold_in(own, 2), (rows, 1), 0, top)
    return jnp.take_along_axis(table, (jnp.arange(top)[None, :] + turn) % top, axis=1)


def shares(amount, total, limit, lean, full):
    weights = [(1 << 20) // math.isqrt(standing ** lean) + 1 for standing in range(1, amount + 1)]
    largest = limit if full else min(limit, max(-(-total // amount), total * weights[0] // sum(weights)))
    least = 1 if total - largest >= amount - 1 else 0
    given, surplus = [largest] + [least] * (amount - 1), total - largest - least * (amount - 1)
    while surplus > 0:
        movable = [i for i in range(1, amount) if given[i] < largest] or [i for i in range(1, amount) if given[i] < limit]
        pool, budget = sum([weights[i] for i in movable]), surplus
        for i in movable:
            addition = min(limit - given[i], max(1, budget * weights[i] // pool), surplus)
            given[i] = given[i] + addition
            surplus = surplus - addition
    return np.array(given)


def gaussian(stream_key, shape, width, reach, split=(), held_as=jnp.bfloat16):
    entries = width * jax.random.normal(stream_key, shape, jnp.float32)
    if split:
        entries = entries * levels(stream_key, shape, split, -0.22, 0.18)
    return jnp.clip(entries, -reach, reach).astype(held_as)


def setup_inputs(seed: int = 0, part: int = 0) -> dict:
    arg_keys = jax.random.split(jax.random.key(seed), 10)
    own_keys = jax.random.split(jax.random.fold_in(arg_keys[9], part), 10)
    tokens = gaussian(own_keys[0], (TOKENS, D), 1.0, 6.0, ((0, 16),))
    expert_ids_keys = jax.random.split(jax.random.fold_in(own_keys[1], 1), TOKENS // TOK_DEV)
    expert_ids_turns = jax.random.permutation(jax.random.fold_in(own_keys[1], 3), TOKENS // TOK_DEV)
    expert_ids = jax.vmap(lambda own, number: shared_out(jax.random.fold_in(own_keys[1], 2), own, number, TOK_DEV, EXPERTS, TOP, CAP, 2))(expert_ids_keys, expert_ids_turns).reshape((TOKENS, TOP))
    gate_weights = jnp.clip(0.5 + 2.0 * jax.random.uniform(own_keys[2], (TOKENS, TOP), jnp.float32) ** levels(own_keys[2], (TOKENS, TOP), ((0, 16),), -0.2, 0.2), 0.5, 2.5)
    w_gate = gaussian(arg_keys[3], (EXPERTS, D, FF), D ** -0.5, 0.0625, ((0, 8), (2, 2)))
    w_up = gaussian(arg_keys[4], (EXPERTS, D, FF), D ** -0.5, 0.0625, ((0, 8), (2, 2)))
    w_down = gaussian(arg_keys[5], (EXPERTS, FF, D), FF ** -0.5, 0.125, ((0, 8), (1, 2)))
    queries = draw_queries(jax.random.fold_in(jax.random.fold_in(arg_keys[9], part), 71), part)
    cache = draw_cache(jax.random.fold_in(jax.random.fold_in(arg_keys[9], part), 71), part)
    lengths = ragged_sizes(own_keys[8], REQUESTS, REQUESTS * CACHE // 2, CACHE, 2).astype(jnp.int32)
    return {"tokens": tokens, "expert_ids": expert_ids, "gate_weights": gate_weights, "w_gate": w_gate, "w_up": w_up, "w_down": w_down, "queries": queries, "cache": cache, "lengths": lengths}


softmax_scale = 1.0 / 192.0 ** 0.5


def reference(tokens, expert_ids, gate_weights, w_gate, w_up, w_down, queries, cache, lengths):
    blocks = TOKENS // TOK_DEV
    routes = TOK_DEV * TOP
    ids = expert_ids.reshape(blocks, routes)
    onehot = (ids[:, :, None] == jnp.arange(EXPERTS, dtype=jnp.int32)[None, None, :]).astype(jnp.int32)
    slots = jnp.sum((jnp.cumsum(onehot, axis=1) - 1) * onehot, axis=2).astype(jnp.int32)
    block_idx = jnp.broadcast_to(jnp.arange(blocks, dtype=jnp.int32)[:, None], ids.shape)
    rows = jnp.repeat(tokens, TOP, axis=0).reshape(blocks, routes, D)
    buffer = jnp.zeros((EXPERTS, blocks, CAP, D), tokens.dtype).at[ids, block_idx, slots].set(rows)
    group = FF // N_DP

    def one_expert(items):
        slab, wg, wu, wd = items
        inputs = slab.reshape(blocks * CAP, D)
        gate = jnp.dot(inputs, wg, preferred_element_type=jnp.float32)
        upper = jnp.dot(inputs, wu, preferred_element_type=jnp.float32)
        hidden = (jax.nn.silu(gate) * upper).astype(jnp.bfloat16)
        hidden = hidden.astype(jnp.float32).reshape(blocks * CAP, N_DP, group)
        parts = jnp.einsum("snf,nfd->snd", hidden, wd.astype(jnp.float32).reshape(N_DP, group, D))
        parts = lax.optimization_barrier(parts.astype(jnp.bfloat16)).astype(jnp.float32)
        return jnp.sum(parts, axis=1).reshape(blocks, CAP, D)

    results = lax.map(one_expert, (buffer, w_gate, w_up, w_down))
    picked = results[ids, block_idx, slots].reshape(TOKENS, TOP, D)
    moe_out = jnp.sum(gate_weights[:, :, None] * picked, axis=1).astype(jnp.bfloat16)

    def one_request(items):
        query, keys, length = items
        scores = jnp.dot(query, keys.T, preferred_element_type=jnp.float32) * softmax_scale
        valid = jnp.arange(CACHE, dtype=jnp.int32)[None, :] < length
        scores = jnp.where(valid, scores, -jnp.inf)
        probs = jax.nn.softmax(scores, axis=-1).astype(jnp.bfloat16)
        return jnp.dot(probs, keys[:, :LATENT], preferred_element_type=jnp.float32).astype(jnp.bfloat16)

    attn_out = lax.map(one_request, (queries, cache, lengths))
    return moe_out, attn_out
```

```python
import functools

import jax
import jax.numpy as jnp
from jax import lax
from jax.experimental import pallas as pl
from jax.experimental.pallas import tpu as pltpu
from jax.sharding import PartitionSpec as P

ROPE = 64
CORES = 2
MIB = 1 << 20

softmax_scale = 1.0 / 192.0**0.5


def expert_rows(inputs, w_gate, w_up, w_down):
    gate = jnp.dot(inputs, w_gate[0], preferred_element_type=jnp.float32)
    upper = jnp.dot(inputs, w_up[0], preferred_element_type=jnp.float32)
    hidden = (jax.nn.silu(gate) * upper).astype(jnp.bfloat16)
    return jnp.dot(hidden, w_down[0], preferred_element_type=jnp.float32)


def attend(queries, cache, lengths):
    width = cache.shape[1]
    latent = cache.shape[2] - ROPE
    scores = (
        jnp.einsum("rhc,rlc->rhl", queries, cache, preferred_element_type=jnp.float32)
        * softmax_scale
    )
    valid = jnp.arange(width, dtype=jnp.int32)[None, None, :] < lengths[:, None, None]
    scores = jnp.where(valid, scores, -jnp.inf)
    probs = jax.nn.softmax(scores, axis=-1).astype(jnp.bfloat16)
    return jnp.einsum(
        "rhl,rlc->rhc", probs, cache[:, :, :latent], preferred_element_type=jnp.float32
    ).astype(jnp.bfloat16)


def plain(tokens, expert_ids, gate_weights, w_gate, w_up, w_down, queries, cache, lengths):
    n_ep = lax.axis_size("ep")
    n_dp = lax.axis_size("dp")
    tok_rows = tokens.shape[0]
    width = tokens.shape[1]
    top = expert_ids.shape[1]
    capacity = slots_per_expert(tok_rows, top, n_ep)
    flat_ids = expert_ids.reshape(-1)
    onehot = (flat_ids[:, None] == jnp.arange(n_ep, dtype=jnp.int32)[None, :]).astype(jnp.int32)
    slots = jnp.sum((jnp.cumsum(onehot, axis=0) - 1) * onehot, axis=1)
    target = (flat_ids * capacity + slots).reshape(tok_rows, top)
    places = jnp.arange(n_ep * capacity, dtype=jnp.int32)[:, None, None]
    selector = jnp.sum((places == target[None, :, :]).astype(jnp.bfloat16), axis=2)
    buffer = jnp.dot(selector, tokens, preferred_element_type=jnp.float32).astype(jnp.bfloat16)
    spread = jnp.broadcast_to(
        buffer.reshape(n_ep, 1, capacity, width), (n_ep, n_dp, capacity, width)
    )
    arrived = lax.all_to_all(
        spread.reshape(n_ep * n_dp, capacity, width),
        ("ep", "dp"),
        split_axis=0,
        concat_axis=0,
        tiled=True,
    )
    partial_out = expert_rows(arrived.reshape(-1, width), w_gate, w_up, w_down).astype(jnp.bfloat16)
    returned = lax.all_to_all(
        partial_out.reshape(arrived.shape), ("ep", "dp"), split_axis=0, concat_axis=0, tiled=True
    )
    combined = jnp.sum(returned.reshape(n_ep, n_dp, capacity, width), axis=1, dtype=jnp.float32)
    picked = combined.reshape(n_ep * capacity, width)[target]
    moe_out = jnp.sum(gate_weights[:, :, None] * picked, axis=1).astype(jnp.bfloat16)
    attn_out = attend(queries, cache, lengths)
    return (moe_out, attn_out)


def slots_per_expert(tok_rows, top, n_ep):
    return (3 * tok_rows * top + 2 * n_ep - 1) // (2 * n_ep)


def iota(shape, dim):
    return lax.broadcasted_iota(jnp.int32, shape, dim)


def split(value, *sizes):
    digits = []
    for size in reversed(sizes):
        digits.append(lax.rem(value, size))
        value = lax.div(value, size)
    return [value] + digits[::-1]


def ones(mask):
    return jnp.where(mask, 1.0, 0.0).astype(jnp.bfloat16)


def dot(a, b):
    return jnp.dot(a, b, preferred_element_type=jnp.float32)


def slot_table(ids_ref, chip, chips, pieces, capacity, which=None):
    rows = chips * pieces * CORES * capacity
    top, toks = ids_ref.shape
    away, piece, core, slot = split(iota((rows, toks), 0), pieces, CORES, capacity)
    expert = (chip ^ away) * CORES + core
    named = [ids_ref[k : k + 1, :] == expert for k in range(top)]
    any_named = functools.reduce(jnp.logical_or, named)
    before = ones(iota((toks, toks), 0) < iota((toks, toks), 1))
    rank = dot(ones(any_named), before)
    return (any_named if which is None else named[which]) & (rank == slot.astype(jnp.float32))


def spread_pieces(table, chips, pieces, capacity):
    rows, toks = table.shape
    repeat = ones(iota((toks, pieces * toks), 0) == lax.rem(iota((toks, pieces * toks), 1), toks))
    wide = dot(ones(table), repeat)
    _, piece, _, _ = split(iota(wide.shape, 0), pieces, CORES, capacity)
    return jnp.where(piece == lax.div(iota(wide.shape, 1), toks), wide, 0.0).astype(jnp.bfloat16)


def chip_index():
    return lax.div(lax.axis_index("ep"), CORES)


def core_index():
    return lax.rem(lax.axis_index("ep"), CORES)


def pack_kernel(pieces, capacity, ids_ref, tok_ref, *outs):
    chips = len(outs)
    wide = tok_ref.shape[1] // pieces
    table = slot_table(ids_ref, chip_index(), chips, pieces, capacity)
    select = spread_pieces(table, chips, pieces, capacity)
    toks = tok_ref[...].astype(jnp.float32)
    stacked = jnp.concatenate(
        [toks[:, k * wide : (k + 1) * wide] for k in range(pieces)], axis=0
    ).astype(jnp.bfloat16)
    packed = dot(select, stacked).astype(jnp.bfloat16)
    rows = outs[0].shape[0]
    for d, out in enumerate(outs):
        out[...] = packed[d * rows : (d + 1) * rows]


def near_kernel(far_pieces, near_pieces, capacity, chips, *refs):
    ins, (same, other, stack) = refs[:chips], refs[chips:]
    rows = ins[0].shape[0]
    for d, ref in enumerate(ins):
        stack[d * rows : (d + 1) * rows] = ref[...]
    ratio = far_pieces // near_pieces
    wide = ins[0].shape[1]
    shape = (same.shape[0], stack.shape[0])
    piece, away, slot = split(iota(shape, 0), chips, capacity)
    from_away, from_piece, from_core, from_slot = split(iota(shape, 1), far_pieces, CORES, capacity)
    match = (away == from_away) & (slot == from_slot)
    for out, core in ((same, core_index()), (other, 1 - core_index())):
        for h in range(ratio):
            pick = ones(match & (from_core == core) & (from_piece == piece * ratio + h))
            out[:, h * wide : (h + 1) * wide] = dot(pick, stack[...]).astype(jnp.bfloat16)


def expert_kernel(pieces, *refs):
    ins, (w_gate, w_up, w_down), outs, (stack, hidden) = refs[:4], refs[4:7], refs[7:11], refs[11:]
    rows, wide = ins[0].shape
    part = rows // pieces
    total = 4 * part
    for s, ref in enumerate(ins):
        stack[s * rows : (s + 1) * rows] = ref[...]
    shape = (total, 4 * rows)
    who, which = split(iota(shape, 0), part)
    from_who, from_piece, from_which = split(iota(shape, 1), pieces, part)
    match = (who == from_who) & (which == from_which)
    gate = up = None
    for k in range(pieces):
        x = dot(ones(match & (from_piece == k)), stack[...]).astype(jnp.bfloat16)
        g = dot(x, w_gate[k * wide : (k + 1) * wide, :])
        u = dot(x, w_up[k * wide : (k + 1) * wide, :])
        gate, up = (g, u) if gate is None else (gate + g, up + u)
    hidden[...] = (gate / (1.0 + jnp.exp(-gate)) * up).astype(jnp.bfloat16)
    for k in range(pieces):
        stack[k * total : (k + 1) * total] = dot(
            hidden[...], w_down[:, k * wide : (k + 1) * wide]
        ).astype(jnp.bfloat16)
    shape = (4 * rows, pieces * total)
    who, piece, which = split(iota(shape, 0), pieces, part)
    from_piece, from_who, from_which = split(iota(shape, 1), 4, part)
    back = dot(
        ones((who == from_who) & (piece == from_piece) & (which == from_which)), stack[...]
    ).astype(jnp.bfloat16)
    for s, out in enumerate(outs):
        out[...] = back[s * rows : (s + 1) * rows]


def sum_kernel(far_pieces, near_pieces, capacity, chips, own, along, core_ref, across, *refs):
    outs, (stack,) = refs[:chips], refs[chips:]
    rows = own.shape[0]
    ratio = far_pieces // near_pieces
    wide = outs[0].shape[1]
    f32 = jnp.float32
    stack[:rows] = (own[...].astype(f32) + along[...].astype(f32)).astype(jnp.bfloat16)
    stack[rows:] = (core_ref[...].astype(f32) + across[...].astype(f32)).astype(jnp.bfloat16)
    far_rows = outs[0].shape[0]
    shape = (chips * far_rows, 2 * rows)
    away, piece, core, slot = split(iota(shape, 0), far_pieces, CORES, capacity)
    from_other, from_piece, from_away, from_slot = split(
        iota(shape, 1), near_pieces, chips, capacity
    )
    match = (
        (away == from_away)
        & (slot == from_slot)
        & ((core != core_index()) == (from_other == 1))
        & (lax.div(piece, ratio) == from_piece)
    )
    sent = None
    for h in range(ratio):
        term = dot(
            ones(match & (lax.rem(piece, ratio) == h)), stack[:, h * wide : (h + 1) * wide]
        )
        sent = term if sent is None else sent + term
    sent = sent.astype(jnp.bfloat16)
    for d, out in enumerate(outs):
        out[...] = sent[d * far_rows : (d + 1) * far_rows]


def combine_kernel(pieces, capacity, chips, ids_ref, gains_ref, *refs):
    ins, (out, stack) = refs[:chips], refs[chips:]
    rows, wide = ins[0].shape
    top, toks = ids_ref.shape
    for d, ref in enumerate(ins):
        stack[d * rows : (d + 1) * rows] = ref[...]
    eye = iota((toks, toks), 0) == iota((toks, toks), 1)
    total = None
    for k in range(top):
        table = slot_table(ids_ref, chip_index(), chips, pieces, capacity, k)
        select = spread_pieces(table, chips, pieces, capacity)
        picked = lax.dot_general(
            select, stack[...], (((0,), (0,)), ((), ())), preferred_element_type=jnp.float32
        )
        gain = jnp.sum(jnp.where(eye, gains_ref[k : k + 1, :], 0.0), axis=1, keepdims=True)
        terms = [picked[p * toks : (p + 1) * toks] * gain for p in range(pieces)]
        total = terms if total is None else [a + b for a, b in zip(total, terms)]
    for p in range(pieces):
        out[:, p * wide : (p + 1) * wide] = total[p].astype(jnp.bfloat16)


def start_copies(pairs, sems, cuts):
    copies = []
    for i, (src, dst) in enumerate(pairs):
        rows = src.shape[0] // cuts
        for j in range(cuts):
            span = pl.ds(j * rows, rows)
            copy = pltpu.make_async_copy(src.at[span], dst.at[span], sems.at[i * cuts + j])
            copy.start()
            copies.append(copy)
    return copies


def fetch_kernel(cuts, after, w_gate, w_up, got_gate, got_up, sems):
    del after
    for copy in start_copies([(w_gate, got_gate), (w_up, got_up)], sems, cuts):
        copy.wait()


def attend_kernel(cuts, latent, after, lengths, w_down, queries, cache, got_down, out, sems):
    del after
    copies = start_copies([(w_down, got_down)], sems, cuts)
    requests, _, heads = queries.shape
    width = cache.shape[2]
    for r in range(requests):
        scores = (
            lax.dot_general(
                queries[r], cache[r], (((0,), (0,)), ((), ())), preferred_element_type=jnp.float32
            )
            * softmax_scale
        )
        scores = jnp.where(iota((heads, width), 1) < lengths[r], scores, -jnp.inf)
        weights = jnp.exp(scores - jnp.max(scores, axis=1, keepdims=True))
        probs = (weights / jnp.sum(weights, axis=1, keepdims=True)).astype(jnp.bfloat16)
        out[r] = lax.dot_general(
            probs,
            cache[r, :latent, :],
            (((1,), (1,)), ((), ())),
            preferred_element_type=jnp.float32,
        ).astype(jnp.bfloat16)
    for copy in copies:
        copy.wait()


VMEM = pl.BlockSpec(memory_space=pltpu.VMEM)
HBM = pl.BlockSpec(memory_space=pltpu.HBM)
SMEM = pl.BlockSpec(memory_space=pltpu.SMEM)


def call(kernel, name, out_shape, in_specs, out_specs, scratch, limit, args, flops=0, moved=0):
    return pl.pallas_call(
        kernel,
        name=name,
        out_shape=out_shape,
        in_specs=in_specs,
        out_specs=out_specs,
        scratch_shapes=scratch,
        compiler_params=pltpu.CompilerParams(vmem_limit_bytes=limit),
        cost_estimate=pl.CostEstimate(flops=flops, bytes_accessed=moved, transcendentals=0),
    )(*args)


def paired(n_ep, tokens, expert_ids, gate_weights, w_gate, w_up, w_down, queries, cache, lengths):
    chips = n_ep // CORES
    toks, width = tokens.shape
    top = expert_ids.shape[1]
    bf16 = jnp.bfloat16
    capacity = slots_per_expert(toks, top, n_ep)
    far_pieces, near_pieces = 8, 4
    far_rows, near_rows = far_pieces * CORES * capacity, near_pieces * chips * capacity
    far = jax.ShapeDtypeStruct((far_rows, width // far_pieces), bf16)
    near = jax.ShapeDtypeStruct((near_rows, width // near_pieces), bf16)
    w_gate, w_up, w_down = w_gate[0], w_up[0], w_down[0]
    units = w_gate.shape[1]
    ids, gains = expert_ids.T, gate_weights.T

    def to_chip(x, d):
        return lax.ppermute(x, "ep", [(i, i ^ (CORES * d)) for i in range(n_ep)])

    def to_core(x):
        return lax.ppermute(x, "ep", [(i, i ^ 1) for i in range(n_ep)])

    def along_dp(x):
        return lax.ppermute(x, "dp", [(0, 1), (1, 0)])

    def across(x):
        return lax.ppermute(x, ("ep", "dp"), [(i, i ^ 3) for i in range(2 * n_ep)])

    packed = call(
        functools.partial(pack_kernel, far_pieces, capacity),
        "pack", (far,) * chips, [VMEM] * 2, (VMEM,) * chips, [], 4 * MIB, (ids, tokens),
    )
    landed = [packed[0]] + [to_chip(packed[d], d) for d in range(1, chips)]
    cuts = 8
    got_gate, got_up = call(
        functools.partial(fetch_kernel, cuts),
        "fetch",
        (pltpu.VMEM(w_gate.shape, bf16), pltpu.VMEM(w_up.shape, bf16)),
        [HBM] * 3, (VMEM, VMEM), [pltpu.SemaphoreType.DMA((2 * cuts,))], 1 * MIB,
        (packed[0], w_gate, w_up), moved=2 * 2 * w_gate.size,
    )
    same, other = call(
        functools.partial(near_kernel, far_pieces, near_pieces, capacity, chips),
        "near", (near,) * 2, [VMEM] * chips, (VMEM,) * 2,
        [pltpu.VMEM((chips * far_rows, width // far_pieces), bf16)], 4 * MIB, landed,
    )
    arrived = [same, along_dp(same), to_core(other), across(other)]
    latent = cache.shape[2] - ROPE
    got_down, attn_out = call(
        functools.partial(attend_kernel, cuts, latent),
        "attend",
        (
            pltpu.VMEM(w_down.shape, bf16),
            jax.ShapeDtypeStruct(queries.shape[:2] + (latent,), bf16),
        ),
        [HBM, SMEM, HBM, VMEM, VMEM], (VMEM, VMEM), [pltpu.SemaphoreType.DMA((cuts,))], 8 * MIB,
        (same, lengths, w_down, queries.swapaxes(1, 2), cache.swapaxes(1, 2)),
        moved=2 * w_down.size,
    )
    rows = 4 * near_rows // near_pieces
    parts = call(
        functools.partial(expert_kernel, near_pieces),
        "experts", (near,) * 4, [VMEM] * 7, (VMEM,) * 4,
        [pltpu.VMEM((4 * near_rows, width // near_pieces), bf16), pltpu.VMEM((rows, units), bf16)],
        8 * MIB, (*arrived, got_gate, got_up, got_down), flops=6 * rows * width * units,
    )
    sums = call(
        functools.partial(sum_kernel, far_pieces, near_pieces, capacity, chips),
        "sums", (far,) * chips, [VMEM] * 4, (VMEM,) * chips,
        [pltpu.VMEM((2 * near_rows, width // near_pieces), bf16)], 6 * MIB,
        (parts[0], along_dp(parts[1]), to_core(parts[2]), across(parts[3])),
    )
    back = [sums[0]] + [to_chip(sums[d], d) for d in range(1, chips)]
    moe_out = call(
        functools.partial(combine_kernel, far_pieces, capacity, chips),
        "combine", jax.ShapeDtypeStruct(tokens.shape, bf16), [VMEM] * (2 + chips), VMEM,
        [pltpu.VMEM((chips * far_rows, width // far_pieces), bf16)], 4 * MIB, (ids, gains, *back),
    )
    return moe_out, attn_out


def solution(mesh):
    placed = (
        P(("group", "ep", "dp"), None),
        P(("group", "ep", "dp"), None),
        P(("group", "ep", "dp"), None),
        P("ep", None, "dp"),
        P("ep", None, "dp"),
        P("ep", "dp", None),
        P(("group", "ep", "dp"), None, None),
        P(("group", "ep", "dp"), None, None),
        P(("group", "ep", "dp")),
    )
    n_ep, n_dp = mesh.shape["ep"], mesh.shape["dp"]
    fits = n_dp == 2 and n_ep == 8
    return jax.shard_map(
        functools.partial(paired, n_ep) if fits else plain,
        mesh=mesh,
        in_specs=placed,
        out_specs=(P(("group", "ep", "dp"), None), P(("group", "ep", "dp"), None, None)),
        check_vma=False,
    )
```

```python
import functools

import jax
import jax.numpy as jnp
from jax import lax
from jax.experimental import pallas as pl
from jax.experimental.pallas import tpu as pltpu
from jax.sharding import PartitionSpec as P

ROPE = 64
CORES = 2
MIB = 1 << 20

softmax_scale = 1.0 / 192.0**0.5


def expert_rows(inputs, w_gate, w_up, w_down):
    gate = jnp.dot(inputs, w_gate[0], preferred_element_type=jnp.float32)
    upper = jnp.dot(inputs, w_up[0], preferred_element_type=jnp.float32)
    hidden = (jax.nn.silu(gate) * upper).astype(jnp.bfloat16)
    return jnp.dot(hidden, w_down[0], preferred_element_type=jnp.float32)


def attend(queries, cache, lengths):
    width = cache.shape[1]
    latent = cache.shape[2] - ROPE
    scores = (
        jnp.einsum("rhc,rlc->rhl", queries, cache, preferred_element_type=jnp.float32)
        * softmax_scale
    )
    valid = jnp.arange(width, dtype=jnp.int32)[None, None, :] < lengths[:, None, None]
    scores = jnp.where(valid, scores, -jnp.inf)
    probs = jax.nn.softmax(scores, axis=-1).astype(jnp.bfloat16)
    return jnp.einsum(
        "rhl,rlc->rhc", probs, cache[:, :, :latent], preferred_element_type=jnp.float32
    ).astype(jnp.bfloat16)


def plain(tokens, expert_ids, gate_weights, w_gate, w_up, w_down, queries, cache, lengths):
    n_ep = lax.axis_size("ep")
    n_dp = lax.axis_size("dp")
    tok_rows = tokens.shape[0]
    width = tokens.shape[1]
    top = expert_ids.shape[1]
    capacity = slots_per_expert(tok_rows, top, n_ep)
    flat_ids = expert_ids.reshape(-1)
    onehot = (flat_ids[:, None] == jnp.arange(n_ep, dtype=jnp.int32)[None, :]).astype(jnp.int32)
    slots = jnp.sum((jnp.cumsum(onehot, axis=0) - 1) * onehot, axis=1)
    target = (flat_ids * capacity + slots).reshape(tok_rows, top)
    places = jnp.arange(n_ep * capacity, dtype=jnp.int32)[:, None, None]
    selector = jnp.sum((places == target[None, :, :]).astype(jnp.bfloat16), axis=2)
    buffer = jnp.dot(selector, tokens, preferred_element_type=jnp.float32).astype(jnp.bfloat16)
    spread = jnp.broadcast_to(
        buffer.reshape(n_ep, 1, capacity, width), (n_ep, n_dp, capacity, width)
    )
    arrived = lax.all_to_all(
        spread.reshape(n_ep * n_dp, capacity, width),
        ("ep", "dp"),
        split_axis=0,
        concat_axis=0,
        tiled=True,
    )
    partial_out = expert_rows(arrived.reshape(-1, width), w_gate, w_up, w_down).astype(jnp.bfloat16)
    returned = lax.all_to_all(
        partial_out.reshape(arrived.shape), ("ep", "dp"), split_axis=0, concat_axis=0, tiled=True
    )
    combined = jnp.sum(returned.reshape(n_ep, n_dp, capacity, width), axis=1, dtype=jnp.float32)
    picked = combined.reshape(n_ep * capacity, width)[target]
    moe_out = jnp.sum(gate_weights[:, :, None] * picked, axis=1).astype(jnp.bfloat16)
    attn_out = attend(queries, cache, lengths)
    return (moe_out, attn_out)


def slots_per_expert(tok_rows, top, n_ep):
    return (3 * tok_rows * top + 2 * n_ep - 1) // (2 * n_ep)


def iota(shape, dim):
    return lax.broadcasted_iota(jnp.int32, shape, dim)


def split(value, *sizes):
    digits = []
    for size in reversed(sizes):
        digits.append(lax.rem(value, size))
        value = lax.div(value, size)
    return [value] + digits[::-1]


def ones(mask):
    return jnp.where(mask, 1.0, 0.0).astype(jnp.bfloat16)


def dot(a, b):
    return jnp.dot(a, b, preferred_element_type=jnp.float32)


def slot_table(ids_ref, chip, chips, pieces, capacity, which=None):
    rows = chips * pieces * CORES * capacity
    top, toks = ids_ref.shape
    away, piece, core, slot = split(iota((rows, toks), 0), pieces, CORES, capacity)
    expert = (chip ^ away) * CORES + core
    named = [ids_ref[k : k + 1, :] == expert for k in range(top)]
    any_named = functools.reduce(jnp.logical_or, named)
    before = ones(iota((toks, toks), 0) < iota((toks, toks), 1))
    rank = dot(ones(any_named), before)
    return (any_named if which is None else named[which]) & (rank == slot.astype(jnp.float32))


def spread_pieces(table, chips, pieces, capacity):
    rows, toks = table.shape
    repeat = ones(iota((toks, pieces * toks), 0) == lax.rem(iota((toks, pieces * toks), 1), toks))
    wide = dot(ones(table), repeat)
    _, piece, _, _ = split(iota(wide.shape, 0), pieces, CORES, capacity)
    return jnp.where(piece == lax.div(iota(wide.shape, 1), toks), wide, 0.0).astype(jnp.bfloat16)


def chip_index():
    return lax.div(lax.axis_index("ep"), CORES)


def core_index():
    return lax.rem(lax.axis_index("ep"), CORES)


def pack_kernel(pieces, capacity, ids_ref, tok_ref, *outs):
    chips = len(outs)
    wide = tok_ref.shape[1] // pieces
    table = slot_table(ids_ref, chip_index(), chips, pieces, capacity)
    select = spread_pieces(table, chips, pieces, capacity)
    toks = tok_ref[...].astype(jnp.float32)
    stacked = jnp.concatenate(
        [toks[:, k * wide : (k + 1) * wide] for k in range(pieces)], axis=0
    ).astype(jnp.bfloat16)
    packed = dot(select, stacked).astype(jnp.bfloat16)
    rows = outs[0].shape[0]
    for d, out in enumerate(outs):
        out[...] = packed[d * rows : (d + 1) * rows]


def near_kernel(far_pieces, near_pieces, capacity, chips, *refs):
    ins, (same, other, stack) = refs[:chips], refs[chips:]
    rows = ins[0].shape[0]
    for d, ref in enumerate(ins):
        stack[d * rows : (d + 1) * rows] = ref[...]
    ratio = far_pieces // near_pieces
    wide = ins[0].shape[1]
    shape = (same.shape[0], stack.shape[0])
    piece, away, slot = split(iota(shape, 0), chips, capacity)
    from_away, from_piece, from_core, from_slot = split(iota(shape, 1), far_pieces, CORES, capacity)
    match = (away == from_away) & (slot == from_slot)
    for out, core in ((same, core_index()), (other, 1 - core_index())):
        for h in range(ratio):
            pick = ones(match & (from_core == core) & (from_piece == piece * ratio + h))
            out[:, h * wide : (h + 1) * wide] = dot(pick, stack[...]).astype(jnp.bfloat16)


def expert_kernel(pieces, *refs):
    ins, (w_gate, w_up, w_down), outs, (stack, hidden) = refs[:4], refs[4:7], refs[7:11], refs[11:]
    rows, wide = ins[0].shape
    part = rows // pieces
    total = 4 * part
    for s, ref in enumerate(ins):
        stack[s * rows : (s + 1) * rows] = ref[...]
    shape = (total, 4 * rows)
    who, which = split(iota(shape, 0), part)
    from_who, from_piece, from_which = split(iota(shape, 1), pieces, part)
    match = (who == from_who) & (which == from_which)
    gate = up = None
    for k in range(pieces):
        x = dot(ones(match & (from_piece == k)), stack[...]).astype(jnp.bfloat16)
        g = dot(x, w_gate[k * wide : (k + 1) * wide, :])
        u = dot(x, w_up[k * wide : (k + 1) * wide, :])
        gate, up = (g, u) if gate is None else (gate + g, up + u)
    hidden[...] = (gate / (1.0 + jnp.exp(-gate)) * up).astype(jnp.bfloat16)
    for k in range(pieces):
        stack[k * total : (k + 1) * total] = dot(
            hidden[...], w_down[:, k * wide : (k + 1) * wide]
        ).astype(jnp.bfloat16)
    shape = (4 * rows, pieces * total)
    who, piece, which = split(iota(shape, 0), pieces, part)
    from_piece, from_who, from_which = split(iota(shape, 1), 4, part)
    back = dot(
        ones((who == from_who) & (piece == from_piece) & (which == from_which)), stack[...]
    ).astype(jnp.bfloat16)
    for s, out in enumerate(outs):
        out[...] = back[s * rows : (s + 1) * rows]


def sum_kernel(far_pieces, near_pieces, capacity, chips, own, along, core_ref, across, *refs):
    outs, (stack,) = refs[:chips], refs[chips:]
    rows = own.shape[0]
    ratio = far_pieces // near_pieces
    wide = outs[0].shape[1]
    f32 = jnp.float32
    stack[:rows] = (own[...].astype(f32) + along[...].astype(f32)).astype(jnp.bfloat16)
    stack[rows:] = (core_ref[...].astype(f32) + across[...].astype(f32)).astype(jnp.bfloat16)
    far_rows = outs[0].shape[0]
    shape = (chips * far_rows, 2 * rows)
    away, piece, core, slot = split(iota(shape, 0), far_pieces, CORES, capacity)
    from_other, from_piece, from_away, from_slot = split(
        iota(shape, 1), near_pieces, chips, capacity
    )
    match = (
        (away == from_away)
        & (slot == from_slot)
        & ((core != core_index()) == (from_other == 1))
        & (lax.div(piece, ratio) == from_piece)
    )
    sent = None
    for h in range(ratio):
        term = dot(
            ones(match & (lax.rem(piece, ratio) == h)), stack[:, h * wide : (h + 1) * wide]
        )
        sent = term if sent is None else sent + term
    sent = sent.astype(jnp.bfloat16)
    for d, out in enumerate(outs):
        out[...] = sent[d * far_rows : (d + 1) * far_rows]


def combine_kernel(pieces, capacity, chips, ids_ref, gains_ref, *refs):
    ins, (out, stack) = refs[:chips], refs[chips:]
    rows, wide = ins[0].shape
    top, toks = ids_ref.shape
    for d, ref in enumerate(ins):
        stack[d * rows : (d + 1) * rows] = ref[...]
    eye = iota((toks, toks), 0) == iota((toks, toks), 1)
    total = None
    for k in range(top):
        table = slot_table(ids_ref, chip_index(), chips, pieces, capacity, k)
        select = spread_pieces(table, chips, pieces, capacity)
        picked = lax.dot_general(
            select, stack[...], (((0,), (0,)), ((), ())), preferred_element_type=jnp.float32
        )
        gain = jnp.sum(jnp.where(eye, gains_ref[k : k + 1, :], 0.0), axis=1, keepdims=True)
        terms = [picked[p * toks : (p + 1) * toks] * gain for p in range(pieces)]
        total = terms if total is None else [a + b for a, b in zip(total, terms)]
    for p in range(pieces):
        out[:, p * wide : (p + 1) * wide] = total[p].astype(jnp.bfloat16)


def start_copies(pairs, sems, cuts):
    copies = []
    for i, (src, dst) in enumerate(pairs):
        rows = src.shape[0] // cuts
        for j in range(cuts):
            span = pl.ds(j * rows, rows)
            copy = pltpu.make_async_copy(src.at[span], dst.at[span], sems.at[i * cuts + j])
            copy.start()
            copies.append(copy)
    return copies


def fetch_kernel(cuts, after, w_gate, w_up, got_gate, got_up, sems):
    del after
    for copy in start_copies([(w_gate, got_gate), (w_up, got_up)], sems, cuts):
        copy.wait()


def attend_kernel(cuts, latent, after, lengths, w_down, queries, cache, got_down, out, sems):
    del after
    copies = start_copies([(w_down, got_down)], sems, cuts)
    requests, _, heads = queries.shape
    width = cache.shape[2]
    for r in range(requests):
        scores = (
            lax.dot_general(
                queries[r], cache[r], (((0,), (0,)), ((), ())), preferred_element_type=jnp.float32
            )
            * softmax_scale
        )
        scores = jnp.where(iota((heads, width), 1) < lengths[r], scores, -jnp.inf)
        weights = jnp.exp(scores - jnp.max(scores, axis=1, keepdims=True))
        probs = (weights / jnp.sum(weights, axis=1, keepdims=True)).astype(jnp.bfloat16)
        out[r] = lax.dot_general(
            probs,
            cache[r, :latent, :],
            (((1,), (1,)), ((), ())),
            preferred_element_type=jnp.float32,
        ).astype(jnp.bfloat16)
    for copy in copies:
        copy.wait()


VMEM = pl.BlockSpec(memory_space=pltpu.VMEM)
HBM = pl.BlockSpec(memory_space=pltpu.HBM)
SMEM = pl.BlockSpec(memory_space=pltpu.SMEM)


def call(kernel, name, out_shape, in_specs, out_specs, scratch, limit, args, flops=0, moved=0):
    return pl.pallas_call(
        kernel,
        name=name,
        out_shape=out_shape,
        in_specs=in_specs,
        out_specs=out_specs,
        scratch_shapes=scratch,
        compiler_params=pltpu.CompilerParams(vmem_limit_bytes=limit),
        cost_estimate=pl.CostEstimate(flops=flops, bytes_accessed=moved, transcendentals=0),
    )(*args)


def paired(n_ep, tokens, expert_ids, gate_weights, w_gate, w_up, w_down, queries, cache, lengths):
    chips = n_ep // CORES
    toks, width = tokens.shape
    top = expert_ids.shape[1]
    bf16 = jnp.bfloat16
    capacity = slots_per_expert(toks, top, n_ep)
    far_pieces, near_pieces = 8, 4
    far_rows, near_rows = far_pieces * CORES * capacity, near_pieces * chips * capacity
    far = jax.ShapeDtypeStruct((far_rows, width // far_pieces), bf16)
    near = jax.ShapeDtypeStruct((near_rows, width // near_pieces), bf16)
    w_gate, w_up, w_down = (
        pltpu.with_memory_space_constraint(w[0], pltpu.HBM) for w in (w_gate, w_up, w_down)
    )
    units = w_gate.shape[1]
    ids, gains = expert_ids.T, gate_weights.T

    def to_chip(x, d):
        return lax.ppermute(x, "ep", [(i, i ^ (CORES * d)) for i in range(n_ep)])

    def to_core(x):
        return lax.ppermute(x, "ep", [(i, i ^ 1) for i in range(n_ep)])

    def along_dp(x):
        return lax.ppermute(x, "dp", [(0, 1), (1, 0)])

    def across(x):
        return lax.ppermute(x, ("ep", "dp"), [(i, i ^ 3) for i in range(2 * n_ep)])

    packed = call(
        functools.partial(pack_kernel, far_pieces, capacity),
        "pack", (far,) * chips, [VMEM] * 2, (VMEM,) * chips, [], 4 * MIB, (ids, tokens),
    )
    landed = [packed[0]] + [to_chip(packed[d], d) for d in range(1, chips)]
    cuts = 8
    got_gate, got_up = call(
        functools.partial(fetch_kernel, cuts),
        "fetch",
        (pltpu.VMEM(w_gate.shape, bf16), pltpu.VMEM(w_up.shape, bf16)),
        [HBM] * 3, (VMEM, VMEM), [pltpu.SemaphoreType.DMA((2 * cuts,))], 1 * MIB,
        (packed[0], w_gate, w_up), moved=2 * 2 * w_gate.size,
    )
    same, other = call(
        functools.partial(near_kernel, far_pieces, near_pieces, capacity, chips),
        "near", (near,) * 2, [VMEM] * chips, (VMEM,) * 2,
        [pltpu.VMEM((chips * far_rows, width // far_pieces), bf16)], 2 * MIB, landed,
    )
    arrived = [same, along_dp(same), to_core(other), across(other)]
    latent = cache.shape[2] - ROPE
    got_down, attn_out = call(
        functools.partial(attend_kernel, cuts, latent),
        "attend",
        (
            pltpu.VMEM(w_down.shape, bf16),
            jax.ShapeDtypeStruct(queries.shape[:2] + (latent,), bf16),
        ),
        [HBM, SMEM, HBM, VMEM, VMEM], (VMEM, VMEM), [pltpu.SemaphoreType.DMA((cuts,))], 2 * MIB,
        (same, lengths, w_down, queries.swapaxes(1, 2), cache.swapaxes(1, 2)),
        moved=2 * w_down.size,
    )
    rows = 4 * near_rows // near_pieces
    parts = call(
        functools.partial(expert_kernel, near_pieces),
        "experts", (near,) * 4, [VMEM] * 7, (VMEM,) * 4,
        [pltpu.VMEM((4 * near_rows, width // near_pieces), bf16), pltpu.VMEM((rows, units), bf16)],
        4 * MIB, (*arrived, got_gate, got_up, got_down), flops=6 * rows * width * units,
    )
    sums = call(
        functools.partial(sum_kernel, far_pieces, near_pieces, capacity, chips),
        "sums", (far,) * chips, [VMEM] * 4, (VMEM,) * chips,
        [pltpu.VMEM((2 * near_rows, width // near_pieces), bf16)], 6 * MIB,
        (parts[0], along_dp(parts[1]), to_core(parts[2]), across(parts[3])),
    )
    back = [sums[0]] + [to_chip(sums[d], d) for d in range(1, chips)]
    moe_out = call(
        functools.partial(combine_kernel, far_pieces, capacity, chips),
        "combine", jax.ShapeDtypeStruct(tokens.shape, bf16), [VMEM] * (2 + chips), VMEM,
        [pltpu.VMEM((chips * far_rows, width // far_pieces), bf16)], 4 * MIB, (ids, gains, *back),
    )
    return moe_out, attn_out


def solution(mesh):
    placed = (
        P(("group", "ep", "dp"), None),
        P(("group", "ep", "dp"), None),
        P(("group", "ep", "dp"), None),
        P("ep", None, "dp"),
        P("ep", None, "dp"),
        P("ep", "dp", None),
        P(("group", "ep", "dp"), None, None),
        P(("group", "ep", "dp"), None, None),
        P(("group", "ep", "dp")),
    )
    n_ep, n_dp = mesh.shape["ep"], mesh.shape["dp"]
    fits = n_dp == 2 and n_ep == 8
    return jax.shard_map(
        functools.partial(paired, n_ep) if fits else plain,
        mesh=mesh,
        in_specs=placed,
        out_specs=(P(("group", "ep", "dp"), None), P(("group", "ep", "dp"), None, None)),
        check_vma=False,
    )
```

```python
import functools

import jax
import jax.numpy as jnp
from jax import lax
from jax.experimental import pallas as pl
from jax.experimental.pallas import tpu as pltpu
from jax.sharding import PartitionSpec as P

ROPE = 64
CORES = 2
MIB = 1 << 20

softmax_scale = 1.0 / 192.0**0.5


def expert_rows(inputs, w_gate, w_up, w_down):
    gate = jnp.dot(inputs, w_gate[0], preferred_element_type=jnp.float32)
    upper = jnp.dot(inputs, w_up[0], preferred_element_type=jnp.float32)
    hidden = (jax.nn.silu(gate) * upper).astype(jnp.bfloat16)
    return jnp.dot(hidden, w_down[0], preferred_element_type=jnp.float32)


def attend(queries, cache, lengths):
    width = cache.shape[1]
    latent = cache.shape[2] - ROPE
    scores = (
        jnp.einsum("rhc,rlc->rhl", queries, cache, preferred_element_type=jnp.float32)
        * softmax_scale
    )
    valid = jnp.arange(width, dtype=jnp.int32)[None, None, :] < lengths[:, None, None]
    scores = jnp.where(valid, scores, -jnp.inf)
    probs = jax.nn.softmax(scores, axis=-1).astype(jnp.bfloat16)
    return jnp.einsum(
        "rhl,rlc->rhc", probs, cache[:, :, :latent], preferred_element_type=jnp.float32
    ).astype(jnp.bfloat16)


def plain(tokens, expert_ids, gate_weights, w_gate, w_up, w_down, queries, cache, lengths):
    n_ep = lax.axis_size("ep")
    n_dp = lax.axis_size("dp")
    tok_rows = tokens.shape[0]
    width = tokens.shape[1]
    top = expert_ids.shape[1]
    capacity = slots_per_expert(tok_rows, top, n_ep)
    flat_ids = expert_ids.reshape(-1)
    onehot = (flat_ids[:, None] == jnp.arange(n_ep, dtype=jnp.int32)[None, :]).astype(jnp.int32)
    slots = jnp.sum((jnp.cumsum(onehot, axis=0) - 1) * onehot, axis=1)
    target = (flat_ids * capacity + slots).reshape(tok_rows, top)
    places = jnp.arange(n_ep * capacity, dtype=jnp.int32)[:, None, None]
    selector = jnp.sum((places == target[None, :, :]).astype(jnp.bfloat16), axis=2)
    buffer = jnp.dot(selector, tokens, preferred_element_type=jnp.float32).astype(jnp.bfloat16)
    spread = jnp.broadcast_to(
        buffer.reshape(n_ep, 1, capacity, width), (n_ep, n_dp, capacity, width)
    )
    arrived = lax.all_to_all(
        spread.reshape(n_ep * n_dp, capacity, width),
        ("ep", "dp"),
        split_axis=0,
        concat_axis=0,
        tiled=True,
    )
    partial_out = expert_rows(arrived.reshape(-1, width), w_gate, w_up, w_down).astype(jnp.bfloat16)
    returned = lax.all_to_all(
        partial_out.reshape(arrived.shape), ("ep", "dp"), split_axis=0, concat_axis=0, tiled=True
    )
    combined = jnp.sum(returned.reshape(n_ep, n_dp, capacity, width), axis=1, dtype=jnp.float32)
    picked = combined.reshape(n_ep * capacity, width)[target]
    moe_out = jnp.sum(gate_weights[:, :, None] * picked, axis=1).astype(jnp.bfloat16)
    attn_out = attend(queries, cache, lengths)
    return (moe_out, attn_out)


def slots_per_expert(tok_rows, top, n_ep):
    return (3 * tok_rows * top + 2 * n_ep - 1) // (2 * n_ep)


PIECES = 8


def iota(shape, dim):
    return lax.broadcasted_iota(jnp.int32, shape, dim)


def split(value, *sizes):
    digits = []
    for size in reversed(sizes):
        digits.append(lax.rem(value, size))
        value = lax.div(value, size)
    return [value] + digits[::-1]


def ones(mask):
    return jnp.where(mask, 1.0, 0.0).astype(jnp.bfloat16)


def dot(a, b):
    return jnp.dot(a, b, preferred_element_type=jnp.float32)


def move(mask, rows):
    return dot(ones(mask), rows).astype(jnp.bfloat16)


def below(refs):
    return jnp.concatenate([ref[...] for ref in refs], axis=0)


def chip_index():
    return lax.div(lax.axis_index("ep"), CORES)


def core_index():
    return lax.rem(lax.axis_index("ep"), CORES)


def slot_table(ids, chips, capacity, which=None):
    top, toks = ids.shape
    rows = chips * PIECES * CORES * capacity
    away, piece, core, slot = split(iota((rows, toks), 0), PIECES, CORES, capacity)
    expert = (chip_index() ^ away) * CORES + core
    named = [ids[k : k + 1, :] == expert for k in range(top)]
    any_named = functools.reduce(jnp.logical_or, named)
    before = ones(iota((toks, toks), 0) < iota((toks, toks), 1))
    rank = dot(ones(any_named), before)
    return (any_named if which is None else named[which]) & (rank == slot.astype(jnp.float32))


def spread_pieces(table, chips, capacity):
    rows, toks = table.shape
    repeat = ones(iota((toks, PIECES * toks), 0) == lax.rem(iota((toks, PIECES * toks), 1), toks))
    wide = dot(ones(table), repeat)
    piece = split(iota(wide.shape, 0), PIECES, CORES, capacity)[1]
    return jnp.where(piece == lax.div(iota(wide.shape, 1), toks), wide, 0.0).astype(jnp.bfloat16)


def pack_kernel(capacity, chips, ids_hbm, tok_hbm, *refs):
    outs, (ids_ref, tok_ref, sems) = refs[:chips], refs[chips:]
    copies = [
        pltpu.make_async_copy(ids_hbm, ids_ref, sems.at[0]),
        pltpu.make_async_copy(tok_hbm, tok_ref, sems.at[1]),
    ]
    for copy in copies:
        copy.start()
    copies[0].wait()
    select = spread_pieces(slot_table(ids_ref[...], chips, capacity), chips, capacity)
    copies[1].wait()
    wide = tok_ref.shape[1] // PIECES
    toks = tok_ref[...].astype(jnp.float32)
    stacked = jnp.concatenate(
        [toks[:, k * wide : (k + 1) * wide] for k in range(PIECES)], axis=0
    ).astype(jnp.bfloat16)
    packed = dot(select, stacked).astype(jnp.bfloat16)
    rows = outs[0].shape[0]
    for d, out in enumerate(outs):
        out[...] = packed[d * rows : (d + 1) * rows]


def near_kernel(capacity, batch, after, *refs):
    del after
    ins, (same, other) = refs[:batch], refs[batch:]
    rows = below(ins)
    shape = (same.shape[0], rows.shape[0])
    piece, away, slot = split(iota(shape, 0), batch, capacity)
    from_away, from_piece, from_core, from_slot = split(iota(shape, 1), PIECES, CORES, capacity)
    match = (away == from_away) & (slot == from_slot) & (piece == from_piece)
    same[...] = move(match & (from_core == core_index()), rows)
    other[...] = move(match & (from_core != core_index()), rows)


def expert_kernel(n_in, held, *refs):
    ins, (gate_ref, up_ref, up_hbm, down_hbm), refs = refs[:n_in], refs[n_in : n_in + 4], refs[n_in + 4 :]
    outs, (stack, hidden, up_rest, down_ref, sems) = refs[:n_in], refs[n_in:]
    rows, wide = ins[0].shape
    part = rows // PIECES
    total = n_in * part
    rest = [
        pltpu.make_async_copy(
            up_hbm.at[pl.ds(p * wide, wide)],
            up_rest.at[pl.ds((p - held) * wide, wide)],
            sems.at[p],
        )
        for p in range(held, PIECES)
    ]
    down = [
        pltpu.make_async_copy(
            down_hbm.at[:, pl.ds(p * wide, wide)],
            down_ref.at[:, pl.ds(p * wide, wide)],
            sems.at[PIECES + p],
        )
        for p in range(PIECES)
    ]
    for copy in rest + down:
        copy.start()
    shape = (PIECES * total, n_in * rows)
    piece, who, which = split(iota(shape, 0), n_in, part)
    from_who, from_piece, from_which = split(iota(shape, 1), PIECES, part)
    match = (who == from_who) & (which == from_which) & (piece == from_piece)
    stack[...] = move(match, below(ins))
    gate = up = 0.0
    for p in range(PIECES):
        span = slice(p * wide, (p + 1) * wide)
        gate += dot(stack[p * total : (p + 1) * total], gate_ref[span, :])
    for p in range(PIECES):
        if p < held:
            block = up_ref[p * wide : (p + 1) * wide, :]
        else:
            rest[p - held].wait()
            block = up_rest[(p - held) * wide : (p - held + 1) * wide, :]
        up += dot(stack[p * total : (p + 1) * total], block)
    hidden[...] = (gate / (1.0 + jnp.exp(-gate)) * up).astype(jnp.bfloat16)
    for p in range(PIECES):
        down[p].wait()
        stack[p * total : (p + 1) * total] = dot(
            hidden[...], down_ref[:, p * wide : (p + 1) * wide]
        ).astype(jnp.bfloat16)
    shape = (n_in * rows, PIECES * total)
    who, piece, which = split(iota(shape, 0), PIECES, part)
    from_piece, from_who, from_which = split(iota(shape, 1), n_in, part)
    match = (who == from_who) & (which == from_which) & (piece == from_piece)
    back = move(match, stack[...])
    for s, out in enumerate(outs):
        out[...] = back[s * rows : (s + 1) * rows]


def sum_kernel(capacity, batch, after, own, along, beside, across, *outs):
    del after
    f32 = jnp.float32
    same = own[...].astype(f32) + along[...].astype(f32)
    other = beside[...].astype(f32) + across[...].astype(f32)
    rows = jnp.concatenate([same.astype(jnp.bfloat16), other.astype(jnp.bfloat16)], axis=0)
    far_rows = outs[0].shape[0]
    shape = (batch * far_rows, rows.shape[0])
    away, piece, core, slot = split(iota(shape, 0), PIECES, CORES, capacity)
    from_other, from_piece, from_away, from_slot = split(iota(shape, 1), PIECES, batch, capacity)
    match = (away == from_away) & (slot == from_slot) & (piece == from_piece)
    sent = move(match & ((core != core_index()) == (from_other == 1)), rows)
    for d, out in enumerate(outs):
        out[...] = sent[d * far_rows : (d + 1) * far_rows]


def combine_kernel(chips, picks_ref, gains_ref, *refs):
    ins, out = refs[:chips], refs[chips]
    wide = ins[0].shape[1]
    top, toks = gains_ref.shape
    picked = dot(picks_ref[...], below(ins))
    eye = iota((toks, toks), 0) == iota((toks, toks), 1)
    gains = [
        jnp.sum(jnp.where(eye, gains_ref[k : k + 1, :], 0.0), axis=1, keepdims=True)
        for k in range(top)
    ]
    for p in range(PIECES):
        terms = [
            picked[(k * PIECES + p) * toks : (k * PIECES + p + 1) * toks] * gains[k]
            for k in range(top)
        ]
        out[:, p * wide : (p + 1) * wide] = sum(terms[1:], terms[0]).astype(jnp.bfloat16)


def start_copies(src, dst, sems, cuts):
    rows = dst.shape[0] // cuts
    spans = [pl.ds(j * rows, rows) for j in range(cuts)]
    copies = [
        pltpu.make_async_copy(src.at[span], dst.at[span], sems.at[j]) for j, span in enumerate(spans)
    ]
    for copy in copies:
        copy.start()
    return copies


def fetch_kernel(cuts, after, w_gate, got_gate, done, sems):
    del after
    for copy in start_copies(w_gate, got_gate, sems, cuts):
        copy.wait()
    done[...] = jnp.zeros_like(done)


def attend_kernel(cuts, latent, chips, capacity, after, lengths, ids_ref, w_up, queries, cache, got_up, out, picks, sems):
    del after
    copies = start_copies(w_up, got_up, sems, cuts)
    top, toks = ids_ref.shape
    requests, _, heads = queries.shape
    width = cache.shape[2]
    rows = picks.shape[1]
    eye = ones(iota((rows, rows), 0) == iota((rows, rows), 1))
    for k in range(top):
        select = spread_pieces(slot_table(ids_ref[...], chips, capacity, k), chips, capacity)
        picks[k * PIECES * toks : (k + 1) * PIECES * toks] = lax.dot_general(
            select, eye, (((0,), (0,)), ((), ())), preferred_element_type=jnp.float32
        ).astype(jnp.bfloat16)
    for r in range(requests):
        scores = (
            lax.dot_general(
                queries[r], cache[r], (((0,), (0,)), ((), ())), preferred_element_type=jnp.float32
            )
            * softmax_scale
        )
        scores = jnp.where(iota((heads, width), 1) < lengths[r], scores, -jnp.inf)
        weights = jnp.exp(scores - jnp.max(scores, axis=1, keepdims=True))
        probs = (weights / jnp.sum(weights, axis=1, keepdims=True)).astype(jnp.bfloat16)
        out[r] = lax.dot_general(
            probs,
            cache[r, :latent, :],
            (((1,), (1,)), ((), ())),
            preferred_element_type=jnp.float32,
        ).astype(jnp.bfloat16)
    for copy in copies:
        copy.wait()


VMEM = pl.BlockSpec(memory_space=pltpu.VMEM)
HBM = pl.BlockSpec(memory_space=pltpu.HBM)
SMEM = pl.BlockSpec(memory_space=pltpu.SMEM)
DMA = pltpu.SemaphoreType.DMA


def call(kernel, name, out_shape, in_specs, out_specs, scratch, limit, args, flops=0, moved=0):
    return pl.pallas_call(
        kernel,
        name=name,
        out_shape=out_shape,
        in_specs=in_specs,
        out_specs=out_specs,
        scratch_shapes=scratch,
        compiler_params=pltpu.CompilerParams(vmem_limit_bytes=limit),
        cost_estimate=pl.CostEstimate(flops=flops, bytes_accessed=moved, transcendentals=0),
    )(*args)


def paired(n_ep, tokens, expert_ids, gate_weights, w_gate, w_up, w_down, queries, cache, lengths):
    chips = n_ep // CORES
    batches = [(0, 1), (2, 3)]
    batch = 2
    toks, width = tokens.shape
    top = expert_ids.shape[1]
    bf16 = jnp.bfloat16
    capacity = slots_per_expert(toks, top, n_ep)
    wide = width // PIECES
    far = jax.ShapeDtypeStruct((PIECES * CORES * capacity, wide), bf16)
    near = jax.ShapeDtypeStruct((PIECES * batch * capacity, wide), bf16)
    in_hbm = functools.partial(pltpu.with_memory_space_constraint, memory_space=pltpu.HBM)
    w_gate, w_up, w_down = in_hbm(w_gate[0]), in_hbm(w_up[0]), in_hbm(w_down[0])
    units = w_gate.shape[1]
    ids, gains = expert_ids.T, gate_weights.T

    def to_chip(x, d):
        return lax.ppermute(x, "ep", [(i, i ^ (CORES * d)) for i in range(n_ep)])

    def along(x):
        return lax.ppermute(x, "dp", [(0, 1), (1, 0)])

    def beside(x):
        return lax.ppermute(x, "ep", [(i, i ^ 1) for i in range(n_ep)])

    def across(x):
        return lax.ppermute(x, ("ep", "dp"), [(i, i ^ 3) for i in range(2 * n_ep)])

    packed = call(
        functools.partial(pack_kernel, capacity, chips),
        "pack", (far,) * chips, [HBM] * 2, (VMEM,) * chips,
        [pltpu.VMEM(ids.shape, ids.dtype), pltpu.VMEM(tokens.shape, bf16), DMA((2,))],
        2 * MIB, (in_hbm(ids), in_hbm(tokens)),
    )
    landed = [None] * chips
    landed[0] = packed[0]
    for d in (2, 3, 1):
        landed[d] = to_chip(packed[d], d)
    cuts = 8
    got_gate, token = call(
        functools.partial(fetch_kernel, cuts),
        "fetch", (pltpu.VMEM(w_gate.shape, bf16), jax.ShapeDtypeStruct((8, 128), jnp.float32)),
        [HBM] * 2, (VMEM, VMEM), [DMA((cuts,))], 1 * MIB, (packed[0], w_gate), moved=2 * w_gate.size,
    )
    arrived = []
    for chosen in batches:
        same, other = call(
            functools.partial(near_kernel, capacity, batch),
            "near", (near,) * 2, [HBM] + [VMEM] * batch, (VMEM,) * 2, [], 1 * MIB,
            (token, *[landed[d] for d in chosen]),
        )
        token = same
        arrived += [same, along(same), beside(other), across(other)]
    latent = cache.shape[2] - ROPE
    held = PIECES // 2
    picks_shape = (top * PIECES * toks, chips * far.shape[0])
    got_up, attn_out, picks = call(
        functools.partial(attend_kernel, held, latent, chips, capacity),
        "attend",
        (
            pltpu.VMEM((held * wide, units), bf16),
            jax.ShapeDtypeStruct(queries.shape[:2] + (latent,), bf16),
            jax.ShapeDtypeStruct(picks_shape, bf16),
        ),
        [HBM, SMEM, VMEM, HBM, VMEM, VMEM], (VMEM,) * 3, [DMA((held,))], 2 * MIB,
        (token, lengths, ids, w_up, queries.swapaxes(1, 2), cache.swapaxes(1, 2)),
        moved=held * wide * units * 2,
    )
    n_in = len(arrived)
    rows = n_in * batch * capacity
    parts = call(
        functools.partial(expert_kernel, n_in, held),
        "experts", (near,) * n_in, [VMEM] * (n_in + 2) + [HBM] * 2, (VMEM,) * n_in,
        [
            pltpu.VMEM((PIECES * rows, wide), bf16),
            pltpu.VMEM((rows, units), bf16),
            pltpu.VMEM(((PIECES - held) * wide, units), bf16),
            pltpu.VMEM(w_down.shape, bf16),
            DMA((2 * PIECES,)),
        ],
        28 * MIB, (*arrived, got_gate, got_up, w_up, w_down), flops=6 * rows * width * units,
    )
    back = [None] * chips
    token = picks
    for b in reversed(range(len(batches))):
        own, x, core, diagonal = parts[4 * b : 4 * b + 4]
        sums = call(
            functools.partial(sum_kernel, capacity, batch),
            "sums", (far,) * batch, [HBM] + [VMEM] * 4, (VMEM,) * batch, [], 1 * MIB,
            (token, own, along(x), beside(core), across(diagonal)),
        )
        token = sums[0]
        for d, value in zip(batches[b], sums):
            back[d] = to_chip(value, d) if d else value
    moe_out = call(
        functools.partial(combine_kernel, chips),
        "combine", jax.ShapeDtypeStruct(tokens.shape, bf16), [VMEM] * (2 + chips), VMEM, [],
        4 * MIB, (picks, gains, *back),
    )
    return moe_out, attn_out


def solution(mesh):
    placed = (
        P(("group", "ep", "dp"), None),
        P(("group", "ep", "dp"), None),
        P(("group", "ep", "dp"), None),
        P("ep", None, "dp"),
        P("ep", None, "dp"),
        P("ep", "dp", None),
        P(("group", "ep", "dp"), None, None),
        P(("group", "ep", "dp"), None, None),
        P(("group", "ep", "dp")),
    )
    n_ep, n_dp = mesh.shape["ep"], mesh.shape["dp"]
    fits = n_dp == 2 and n_ep == 8
    return jax.shard_map(
        functools.partial(paired, n_ep) if fits else plain,
        mesh=mesh,
        in_specs=placed,
        out_specs=(P(("group", "ep", "dp"), None), P(("group", "ep", "dp"), None, None)),
        check_vma=False,
    )
```

```python
import functools

import jax
import jax.numpy as jnp
from jax import lax
from jax.experimental import pallas as pl
from jax.experimental.pallas import tpu as pltpu
from jax.sharding import PartitionSpec as P

ROPE = 64
CORES = 2
MIB = 1 << 20

softmax_scale = 1.0 / 192.0**0.5


def expert_rows(inputs, w_gate, w_up, w_down):
    gate = jnp.dot(inputs, w_gate[0], preferred_element_type=jnp.float32)
    upper = jnp.dot(inputs, w_up[0], preferred_element_type=jnp.float32)
    hidden = (jax.nn.silu(gate) * upper).astype(jnp.bfloat16)
    return jnp.dot(hidden, w_down[0], preferred_element_type=jnp.float32)


def attend(queries, cache, lengths):
    width = cache.shape[1]
    latent = cache.shape[2] - ROPE
    scores = (
        jnp.einsum("rhc,rlc->rhl", queries, cache, preferred_element_type=jnp.float32)
        * softmax_scale
    )
    valid = jnp.arange(width, dtype=jnp.int32)[None, None, :] < lengths[:, None, None]
    scores = jnp.where(valid, scores, -jnp.inf)
    probs = jax.nn.softmax(scores, axis=-1).astype(jnp.bfloat16)
    return jnp.einsum(
        "rhl,rlc->rhc", probs, cache[:, :, :latent], preferred_element_type=jnp.float32
    ).astype(jnp.bfloat16)


def plain(tokens, expert_ids, gate_weights, w_gate, w_up, w_down, queries, cache, lengths):
    n_ep = lax.axis_size("ep")
    n_dp = lax.axis_size("dp")
    tok_rows = tokens.shape[0]
    width = tokens.shape[1]
    top = expert_ids.shape[1]
    capacity = slots_per_expert(tok_rows, top, n_ep)
    flat_ids = expert_ids.reshape(-1)
    onehot = (flat_ids[:, None] == jnp.arange(n_ep, dtype=jnp.int32)[None, :]).astype(jnp.int32)
    slots = jnp.sum((jnp.cumsum(onehot, axis=0) - 1) * onehot, axis=1)
    target = (flat_ids * capacity + slots).reshape(tok_rows, top)
    places = jnp.arange(n_ep * capacity, dtype=jnp.int32)[:, None, None]
    selector = jnp.sum((places == target[None, :, :]).astype(jnp.bfloat16), axis=2)
    buffer = jnp.dot(selector, tokens, preferred_element_type=jnp.float32).astype(jnp.bfloat16)
    spread = jnp.broadcast_to(
        buffer.reshape(n_ep, 1, capacity, width), (n_ep, n_dp, capacity, width)
    )
    arrived = lax.all_to_all(
        spread.reshape(n_ep * n_dp, capacity, width),
        ("ep", "dp"),
        split_axis=0,
        concat_axis=0,
        tiled=True,
    )
    partial_out = expert_rows(arrived.reshape(-1, width), w_gate, w_up, w_down).astype(jnp.bfloat16)
    returned = lax.all_to_all(
        partial_out.reshape(arrived.shape), ("ep", "dp"), split_axis=0, concat_axis=0, tiled=True
    )
    combined = jnp.sum(returned.reshape(n_ep, n_dp, capacity, width), axis=1, dtype=jnp.float32)
    picked = combined.reshape(n_ep * capacity, width)[target]
    moe_out = jnp.sum(gate_weights[:, :, None] * picked, axis=1).astype(jnp.bfloat16)
    attn_out = attend(queries, cache, lengths)
    return (moe_out, attn_out)


def slots_per_expert(tok_rows, top, n_ep):
    return (3 * tok_rows * top + 2 * n_ep - 1) // (2 * n_ep)


PIECES = 8
FETCHED = (4, 4)


def iota(shape, dim):
    return lax.broadcasted_iota(jnp.int32, shape, dim)


def split(value, *sizes):
    digits = []
    for size in reversed(sizes):
        digits.append(lax.rem(value, size))
        value = lax.div(value, size)
    return [value] + digits[::-1]


def ones(mask):
    return jnp.where(mask, 1.0, 0.0).astype(jnp.bfloat16)


def dot(a, b):
    return jnp.dot(a, b, preferred_element_type=jnp.float32)


def move(mask, rows):
    return dot(ones(mask), rows).astype(jnp.bfloat16)


def below(refs):
    return jnp.concatenate([ref[...] for ref in refs], axis=0)


def chip_index():
    return lax.div(lax.axis_index("ep"), CORES)


def core_index():
    return lax.rem(lax.axis_index("ep"), CORES)


def slot_table(ids, chips, capacity, which=None):
    top, toks = ids.shape
    rows = chips * PIECES * CORES * capacity
    away, piece, core, slot = split(iota((rows, toks), 0), PIECES, CORES, capacity)
    expert = (chip_index() ^ away) * CORES + core
    named = [ids[k : k + 1, :] == expert for k in range(top)]
    any_named = functools.reduce(jnp.logical_or, named)
    before = ones(iota((toks, toks), 0) < iota((toks, toks), 1))
    rank = dot(ones(any_named), before)
    return (any_named if which is None else named[which]) & (rank == slot.astype(jnp.float32))


def spread_pieces(table, chips, capacity):
    rows, toks = table.shape
    repeat = ones(iota((toks, PIECES * toks), 0) == lax.rem(iota((toks, PIECES * toks), 1), toks))
    wide = dot(ones(table), repeat)
    piece = split(iota(wide.shape, 0), PIECES, CORES, capacity)[1]
    return jnp.where(piece == lax.div(iota(wide.shape, 1), toks), wide, 0.0).astype(jnp.bfloat16)


def pack_kernel(capacity, chips, ids_hbm, tok_hbm, *refs):
    outs, (ids_ref, tok_ref, sems) = refs[:chips], refs[chips:]
    copies = [
        pltpu.make_async_copy(ids_hbm, ids_ref, sems.at[0]),
        pltpu.make_async_copy(tok_hbm, tok_ref, sems.at[1]),
    ]
    for copy in copies:
        copy.start()
    copies[0].wait()
    select = spread_pieces(slot_table(ids_ref[...], chips, capacity), chips, capacity)
    copies[1].wait()
    wide = tok_ref.shape[1] // PIECES
    toks = tok_ref[...].astype(jnp.float32)
    stacked = jnp.concatenate(
        [toks[:, k * wide : (k + 1) * wide] for k in range(PIECES)], axis=0
    ).astype(jnp.bfloat16)
    packed = dot(select, stacked).astype(jnp.bfloat16)
    rows = outs[0].shape[0]
    for d, out in enumerate(outs):
        out[...] = packed[d * rows : (d + 1) * rows]


def near_kernel(capacity, batch, after, *refs):
    del after
    ins, (same, other) = refs[:batch], refs[batch:]
    rows = below(ins)
    shape = (same.shape[0], rows.shape[0])
    piece, away, slot = split(iota(shape, 0), batch, capacity)
    from_away, from_piece, from_core, from_slot = split(iota(shape, 1), PIECES, CORES, capacity)
    match = (away == from_away) & (slot == from_slot) & (piece == from_piece)
    same[...] = move(match & (from_core == core_index()), rows)
    other[...] = move(match & (from_core != core_index()), rows)


def expert_kernel(n_in, n_up, *refs):
    ins, gate_ref, ups, refs = refs[:n_in], refs[n_in], refs[n_in + 1 : n_in + 1 + n_up], refs[n_in + 1 + n_up :]
    w_down, outs, (stack, hidden) = refs[0], refs[1 : n_in + 1], refs[n_in + 1 :]
    rows, wide = ins[0].shape
    part = rows // PIECES
    total = n_in * part
    shape = (PIECES * total, n_in * rows)
    piece, who, which = split(iota(shape, 0), n_in, part)
    from_who, from_piece, from_which = split(iota(shape, 1), PIECES, part)
    match = (who == from_who) & (which == from_which) & (piece == from_piece)
    stack[...] = move(match, below(ins))
    blocks = [
        (ref, slice(p * wide, (p + 1) * wide)) for ref in ups for p in range(ref.shape[0] // wide)
    ]
    gate = up = 0.0
    for p in range(PIECES):
        x = stack[p * total : (p + 1) * total]
        gate += dot(x, gate_ref[p * wide : (p + 1) * wide, :])
        ref, span = blocks[p]
        up += dot(x, ref[span, :])
    hidden[...] = (gate / (1.0 + jnp.exp(-gate)) * up).astype(jnp.bfloat16)
    for p in range(PIECES):
        stack[p * total : (p + 1) * total] = dot(
            hidden[...], w_down[:, p * wide : (p + 1) * wide]
        ).astype(jnp.bfloat16)
    shape = (n_in * rows, PIECES * total)
    who, piece, which = split(iota(shape, 0), PIECES, part)
    from_piece, from_who, from_which = split(iota(shape, 1), n_in, part)
    match = (who == from_who) & (which == from_which) & (piece == from_piece)
    back = move(match, stack[...])
    for s, out in enumerate(outs):
        out[...] = back[s * rows : (s + 1) * rows]


def sum_kernel(capacity, batch, after, own, along, beside, across, *outs):
    del after
    f32 = jnp.float32
    same = own[...].astype(f32) + along[...].astype(f32)
    other = beside[...].astype(f32) + across[...].astype(f32)
    rows = jnp.concatenate([same.astype(jnp.bfloat16), other.astype(jnp.bfloat16)], axis=0)
    far_rows = outs[0].shape[0]
    shape = (batch * far_rows, rows.shape[0])
    away, piece, core, slot = split(iota(shape, 0), PIECES, CORES, capacity)
    from_other, from_piece, from_away, from_slot = split(iota(shape, 1), PIECES, batch, capacity)
    match = (away == from_away) & (slot == from_slot) & (piece == from_piece)
    sent = move(match & ((core != core_index()) == (from_other == 1)), rows)
    for d, out in enumerate(outs):
        out[...] = sent[d * far_rows : (d + 1) * far_rows]


def combine_kernel(chips, picks_ref, gains_ref, *refs):
    ins, out = refs[:chips], refs[chips]
    wide = ins[0].shape[1]
    top, toks = gains_ref.shape
    picked = dot(picks_ref[...], below(ins))
    eye = iota((toks, toks), 0) == iota((toks, toks), 1)
    gains = [
        jnp.sum(jnp.where(eye, gains_ref[k : k + 1, :], 0.0), axis=1, keepdims=True)
        for k in range(top)
    ]
    for p in range(PIECES):
        terms = [
            picked[(k * PIECES + p) * toks : (k * PIECES + p + 1) * toks] * gains[k]
            for k in range(top)
        ]
        out[:, p * wide : (p + 1) * wide] = sum(terms[1:], terms[0]).astype(jnp.bfloat16)


def fetch_kernel(start, count, wide, after, weights, got, done, sems):
    del after
    copies = [
        pltpu.make_async_copy(
            weights.at[pl.ds((start + p) * wide, wide)], got.at[pl.ds(p * wide, wide)], sems.at[p]
        )
        for p in range(count)
    ]
    for copy in copies:
        copy.start()
    done[...] = jnp.zeros_like(done)
    for copy in copies:
        copy.wait()


def attend_kernel(chips, capacity, after, lengths, ids_hbm, queries_hbm, cache_hbm, *refs):
    del after
    out_hbm, picks, ids_ref, queries, cache, out, sems = refs
    requests, _, heads = queries.shape
    width = cache.shape[2]
    latent = out.shape[2]
    inward = [pltpu.make_async_copy(ids_hbm, ids_ref, sems.at[0])]
    for r in range(requests):
        inward.append(pltpu.make_async_copy(queries_hbm.at[r], queries.at[r], sems.at[1 + 3 * r]))
        inward.append(pltpu.make_async_copy(cache_hbm.at[r], cache.at[r], sems.at[2 + 3 * r]))
    for copy in inward:
        copy.start()
    inward[0].wait()
    top, toks = ids_ref.shape
    rows = picks.shape[1]
    eye = ones(iota((rows, rows), 0) == iota((rows, rows), 1))
    for k in range(top):
        select = spread_pieces(slot_table(ids_ref[...], chips, capacity, k), chips, capacity)
        picks[k * PIECES * toks : (k + 1) * PIECES * toks] = lax.dot_general(
            select, eye, (((0,), (0,)), ((), ())), preferred_element_type=jnp.float32
        ).astype(jnp.bfloat16)
    outward = []
    for r in range(requests):
        inward[1 + 2 * r].wait()
        inward[2 + 2 * r].wait()
        scores = (
            lax.dot_general(
                queries[r], cache[r], (((0,), (0,)), ((), ())), preferred_element_type=jnp.float32
            )
            * softmax_scale
        )
        scores = jnp.where(iota((heads, width), 1) < lengths[r], scores, -jnp.inf)
        weights = jnp.exp(scores - jnp.max(scores, axis=1, keepdims=True))
        probs = (weights / jnp.sum(weights, axis=1, keepdims=True)).astype(jnp.bfloat16)
        out[r] = lax.dot_general(
            probs,
            cache[r, :latent, :],
            (((1,), (1,)), ((), ())),
            preferred_element_type=jnp.float32,
        ).astype(jnp.bfloat16)
        outward.append(pltpu.make_async_copy(out.at[r], out_hbm.at[r], sems.at[3 + 3 * r]))
        outward[r].start()
    for copy in outward:
        copy.wait()


VMEM = pl.BlockSpec(memory_space=pltpu.VMEM)
HBM = pl.BlockSpec(memory_space=pltpu.HBM)
SMEM = pl.BlockSpec(memory_space=pltpu.SMEM)
DMA = pltpu.SemaphoreType.DMA


def call(kernel, name, out_shape, in_specs, out_specs, scratch, limit, args, flops=0, moved=0):
    return pl.pallas_call(
        kernel,
        name=name,
        out_shape=out_shape,
        in_specs=in_specs,
        out_specs=out_specs,
        scratch_shapes=scratch,
        compiler_params=pltpu.CompilerParams(vmem_limit_bytes=limit),
        cost_estimate=pl.CostEstimate(flops=flops, bytes_accessed=moved, transcendentals=0),
    )(*args)


def paired(n_ep, tokens, expert_ids, gate_weights, w_gate, w_up, w_down, queries, cache, lengths):
    chips = n_ep // CORES
    batches = [(0, 1), (2, 3)]
    batch = 2
    toks, width = tokens.shape
    top = expert_ids.shape[1]
    bf16 = jnp.bfloat16
    capacity = slots_per_expert(toks, top, n_ep)
    wide = width // PIECES
    far = jax.ShapeDtypeStruct((PIECES * CORES * capacity, wide), bf16)
    near = jax.ShapeDtypeStruct((PIECES * batch * capacity, wide), bf16)
    in_hbm = functools.partial(pltpu.with_memory_space_constraint, memory_space=pltpu.HBM)
    got_gate = pltpu.with_memory_space_constraint(w_gate[0], pltpu.VMEM)
    w_up, got_down = in_hbm(w_up[0]), pltpu.with_memory_space_constraint(w_down[0], pltpu.VMEM)
    units = w_up.shape[1]
    ids, gains = in_hbm(expert_ids.T), gate_weights.T

    def to_chip(x, d):
        return lax.ppermute(x, "ep", [(i, i ^ (CORES * d)) for i in range(n_ep)])

    def along(x):
        return lax.ppermute(x, "dp", [(0, 1), (1, 0)])

    def beside(x):
        return lax.ppermute(x, "ep", [(i, i ^ 1) for i in range(n_ep)])

    def across(x):
        return lax.ppermute(x, ("ep", "dp"), [(i, i ^ 3) for i in range(2 * n_ep)])

    packed = call(
        functools.partial(pack_kernel, capacity, chips),
        "pack", (far,) * chips, [HBM] * 2, (VMEM,) * chips,
        [pltpu.VMEM(ids.shape, ids.dtype), pltpu.VMEM(tokens.shape, bf16), DMA((2,))],
        2 * MIB, (ids, in_hbm(tokens)),
    )
    landed = [None] * chips
    landed[0] = packed[0]
    for d in (2, 3, 1):
        landed[d] = to_chip(packed[d], d)
    arrived, got_up = [], []
    token, begin = packed[0], 0
    for chosen, count in zip(batches, FETCHED):
        same, other = call(
            functools.partial(near_kernel, capacity, batch),
            "near", (near,) * 2, [HBM] + [VMEM] * batch, (VMEM,) * 2, [], 1 * MIB,
            (token, *[landed[d] for d in chosen]),
        )
        arrived += [same, along(same), beside(other), across(other)]
        fetched, token = call(
            functools.partial(fetch_kernel, begin, count, wide),
            "fetch",
            (pltpu.VMEM((count * wide, units), bf16), jax.ShapeDtypeStruct((8, 128), jnp.float32)),
            [HBM] * 2, (VMEM, VMEM), [DMA((count,))], 1 * MIB, (same, w_up),
            moved=2 * count * wide * units,
        )
        got_up.append(fetched)
        begin += count
    n_in = len(arrived)
    rows = n_in * batch * capacity
    parts = call(
        functools.partial(expert_kernel, n_in, len(got_up)),
        "experts", (near,) * n_in, [VMEM] * (n_in + 2 + len(got_up)), (VMEM,) * n_in,
        [
            pltpu.VMEM((PIECES * rows, wide), bf16),
            pltpu.VMEM((rows, units), bf16),
        ],
        4 * MIB, (*arrived, got_gate, *got_up, got_down), flops=6 * rows * width * units,
    )
    back = [None] * chips
    token = parts[0]
    for b in reversed(range(len(batches))):
        own, x, core, diagonal = parts[4 * b : 4 * b + 4]
        sums = call(
            functools.partial(sum_kernel, capacity, batch),
            "sums", (far,) * batch, [HBM] + [VMEM] * 4, (VMEM,) * batch, [], 1 * MIB,
            (token, own, along(x), beside(core), across(diagonal)),
        )
        token = sums[0]
        for d, value in zip(batches[b], sums):
            back[d] = to_chip(value, d) if d else value
    latent = cache.shape[2] - ROPE
    queries, cache = in_hbm(queries.swapaxes(1, 2)), in_hbm(cache.swapaxes(1, 2))
    requests, _, heads = queries.shape
    attn_out, picks = call(
        functools.partial(attend_kernel, chips, capacity),
        "attend",
        (
            jax.ShapeDtypeStruct((requests, heads, latent), bf16),
            jax.ShapeDtypeStruct((top * PIECES * toks, chips * far.shape[0]), bf16),
        ),
        [HBM, SMEM] + [HBM] * 3, (HBM, VMEM),
        [
            pltpu.VMEM(ids.shape, ids.dtype),
            pltpu.VMEM(queries.shape, bf16),
            pltpu.VMEM(cache.shape, bf16),
            pltpu.VMEM((requests, heads, latent), bf16),
            DMA((1 + 3 * requests,)),
        ],
        6 * MIB, (token, in_hbm(lengths), ids, queries, cache), moved=2 * cache.size,
    )
    moe_out = call(
        functools.partial(combine_kernel, chips),
        "combine", jax.ShapeDtypeStruct(tokens.shape, bf16), [VMEM] * (2 + chips), VMEM, [],
        4 * MIB, (picks, gains, *back),
    )
    return moe_out, attn_out


def solution(mesh):
    placed = (
        P(("group", "ep", "dp"), None),
        P(("group", "ep", "dp"), None),
        P(("group", "ep", "dp"), None),
        P("ep", None, "dp"),
        P("ep", None, "dp"),
        P("ep", "dp", None),
        P(("group", "ep", "dp"), None, None),
        P(("group", "ep", "dp"), None, None),
        P(("group", "ep", "dp")),
    )
    n_ep, n_dp = mesh.shape["ep"], mesh.shape["dp"]
    fits = n_dp == 2 and n_ep == 8
    return jax.shard_map(
        functools.partial(paired, n_ep) if fits else plain,
        mesh=mesh,
        in_specs=placed,
        out_specs=(P(("group", "ep", "dp"), None), P(("group", "ep", "dp"), None, None)),
        check_vma=False,
    )
```

```python
import functools

import jax
import jax.numpy as jnp
from jax import lax
from jax.experimental import pallas as pl
from jax.experimental.pallas import tpu as pltpu
from jax.sharding import PartitionSpec as P

ROPE = 64
CORES = 2
MIB = 1 << 20

softmax_scale = 1.0 / 192.0**0.5


def expert_rows(inputs, w_gate, w_up, w_down):
    gate = jnp.dot(inputs, w_gate[0], preferred_element_type=jnp.float32)
    upper = jnp.dot(inputs, w_up[0], preferred_element_type=jnp.float32)
    hidden = (jax.nn.silu(gate) * upper).astype(jnp.bfloat16)
    return jnp.dot(hidden, w_down[0], preferred_element_type=jnp.float32)


def attend(queries, cache, lengths):
    width = cache.shape[1]
    latent = cache.shape[2] - ROPE
    scores = (
        jnp.einsum("rhc,rlc->rhl", queries, cache, preferred_element_type=jnp.float32)
        * softmax_scale
    )
    valid = jnp.arange(width, dtype=jnp.int32)[None, None, :] < lengths[:, None, None]
    scores = jnp.where(valid, scores, -jnp.inf)
    probs = jax.nn.softmax(scores, axis=-1).astype(jnp.bfloat16)
    return jnp.einsum(
        "rhl,rlc->rhc", probs, cache[:, :, :latent], preferred_element_type=jnp.float32
    ).astype(jnp.bfloat16)


def plain(tokens, expert_ids, gate_weights, w_gate, w_up, w_down, queries, cache, lengths):
    n_ep = lax.axis_size("ep")
    n_dp = lax.axis_size("dp")
    tok_rows = tokens.shape[0]
    width = tokens.shape[1]
    top = expert_ids.shape[1]
    capacity = slots_per_expert(tok_rows, top, n_ep)
    flat_ids = expert_ids.reshape(-1)
    onehot = (flat_ids[:, None] == jnp.arange(n_ep, dtype=jnp.int32)[None, :]).astype(jnp.int32)
    slots = jnp.sum((jnp.cumsum(onehot, axis=0) - 1) * onehot, axis=1)
    target = (flat_ids * capacity + slots).reshape(tok_rows, top)
    places = jnp.arange(n_ep * capacity, dtype=jnp.int32)[:, None, None]
    selector = jnp.sum((places == target[None, :, :]).astype(jnp.bfloat16), axis=2)
    buffer = jnp.dot(selector, tokens, preferred_element_type=jnp.float32).astype(jnp.bfloat16)
    spread = jnp.broadcast_to(
        buffer.reshape(n_ep, 1, capacity, width), (n_ep, n_dp, capacity, width)
    )
    arrived = lax.all_to_all(
        spread.reshape(n_ep * n_dp, capacity, width),
        ("ep", "dp"),
        split_axis=0,
        concat_axis=0,
        tiled=True,
    )
    partial_out = expert_rows(arrived.reshape(-1, width), w_gate, w_up, w_down).astype(jnp.bfloat16)
    returned = lax.all_to_all(
        partial_out.reshape(arrived.shape), ("ep", "dp"), split_axis=0, concat_axis=0, tiled=True
    )
    combined = jnp.sum(returned.reshape(n_ep, n_dp, capacity, width), axis=1, dtype=jnp.float32)
    picked = combined.reshape(n_ep * capacity, width)[target]
    moe_out = jnp.sum(gate_weights[:, :, None] * picked, axis=1).astype(jnp.bfloat16)
    attn_out = attend(queries, cache, lengths)
    return (moe_out, attn_out)


def slots_per_expert(tok_rows, top, n_ep):
    return (3 * tok_rows * top + 2 * n_ep - 1) // (2 * n_ep)


PIECES = 8
FETCHED = (2, 1, 5)


def iota(shape, dim):
    return lax.broadcasted_iota(jnp.int32, shape, dim)


def split(value, *sizes):
    digits = []
    for size in reversed(sizes):
        digits.append(lax.rem(value, size))
        value = lax.div(value, size)
    return [value] + digits[::-1]


def ones(mask):
    return jnp.where(mask, 1.0, 0.0).astype(jnp.bfloat16)


def dot(a, b):
    return jnp.dot(a, b, preferred_element_type=jnp.float32)


def move(mask, rows):
    return dot(ones(mask), rows).astype(jnp.bfloat16)


def below(refs):
    return jnp.concatenate([ref[...] for ref in refs], axis=0)


def chip_index():
    return lax.div(lax.axis_index("ep"), CORES)


def core_index():
    return lax.rem(lax.axis_index("ep"), CORES)


def slot_table(ids, chips, capacity, which=None):
    top, toks = ids.shape
    rows = chips * PIECES * CORES * capacity
    away, piece, core, slot = split(iota((rows, toks), 0), PIECES, CORES, capacity)
    expert = (chip_index() ^ away) * CORES + core
    named = [ids[k : k + 1, :] == expert for k in range(top)]
    any_named = functools.reduce(jnp.logical_or, named)
    before = ones(iota((toks, toks), 0) < iota((toks, toks), 1))
    rank = dot(ones(any_named), before)
    return (any_named if which is None else named[which]) & (rank == slot.astype(jnp.float32))


def spread_pieces(table, chips, capacity):
    rows, toks = table.shape
    repeat = ones(iota((toks, PIECES * toks), 0) == lax.rem(iota((toks, PIECES * toks), 1), toks))
    wide = dot(ones(table), repeat)
    piece = split(iota(wide.shape, 0), PIECES, CORES, capacity)[1]
    return jnp.where(piece == lax.div(iota(wide.shape, 1), toks), wide, 0.0).astype(jnp.bfloat16)


def pack_kernel(capacity, chips, ids_hbm, tok_hbm, *refs):
    outs, (ids_ref, tok_ref, sems) = refs[:chips], refs[chips:]
    copies = [
        pltpu.make_async_copy(ids_hbm, ids_ref, sems.at[0]),
        pltpu.make_async_copy(tok_hbm, tok_ref, sems.at[1]),
    ]
    for copy in copies:
        copy.start()
    copies[0].wait()
    select = spread_pieces(slot_table(ids_ref[...], chips, capacity), chips, capacity)
    copies[1].wait()
    wide = tok_ref.shape[1] // PIECES
    toks = tok_ref[...].astype(jnp.float32)
    stacked = jnp.concatenate(
        [toks[:, k * wide : (k + 1) * wide] for k in range(PIECES)], axis=0
    ).astype(jnp.bfloat16)
    packed = dot(select, stacked).astype(jnp.bfloat16)
    rows = outs[0].shape[0]
    for d, out in enumerate(outs):
        out[...] = packed[d * rows : (d + 1) * rows]


def near_kernel(capacity, batch, after, *refs):
    del after
    ins, (same, other) = refs[:batch], refs[batch:]
    rows = below(ins)
    shape = (same.shape[0], rows.shape[0])
    piece, away, slot = split(iota(shape, 0), batch, capacity)
    from_away, from_piece, from_core, from_slot = split(iota(shape, 1), PIECES, CORES, capacity)
    match = (away == from_away) & (slot == from_slot) & (piece == from_piece)
    same[...] = move(match & (from_core == core_index()), rows)
    other[...] = move(match & (from_core != core_index()), rows)


def expert_kernel(n_in, n_up, *refs):
    ins, gate_ref, ups, refs = refs[:n_in], refs[n_in], refs[n_in + 1 : n_in + 1 + n_up], refs[n_in + 1 + n_up :]
    w_down, outs, (stack, hidden) = refs[0], refs[1 : n_in + 1], refs[n_in + 1 :]
    rows, wide = ins[0].shape
    part = rows // PIECES
    total = n_in * part
    shape = (PIECES * total, n_in * rows)
    piece, who, which = split(iota(shape, 0), n_in, part)
    from_who, from_piece, from_which = split(iota(shape, 1), PIECES, part)
    match = (who == from_who) & (which == from_which) & (piece == from_piece)
    stack[...] = move(match, below(ins))
    blocks = [
        (ref, slice(p * wide, (p + 1) * wide)) for ref in ups for p in range(ref.shape[0] // wide)
    ]
    gate = up = 0.0
    for p in range(PIECES):
        x = stack[p * total : (p + 1) * total]
        gate += dot(x, gate_ref[p * wide : (p + 1) * wide, :])
        ref, span = blocks[p]
        up += dot(x, ref[span, :])
    hidden[...] = (gate / (1.0 + jnp.exp(-gate)) * up).astype(jnp.bfloat16)
    for p in range(PIECES):
        stack[p * total : (p + 1) * total] = dot(
            hidden[...], w_down[:, p * wide : (p + 1) * wide]
        ).astype(jnp.bfloat16)
    shape = (n_in * rows, PIECES * total)
    who, piece, which = split(iota(shape, 0), PIECES, part)
    from_piece, from_who, from_which = split(iota(shape, 1), n_in, part)
    match = (who == from_who) & (which == from_which) & (piece == from_piece)
    back = move(match, stack[...])
    for s, out in enumerate(outs):
        out[...] = back[s * rows : (s + 1) * rows]


def sum_kernel(capacity, batch, after, own, along, beside, across, *outs):
    del after
    f32 = jnp.float32
    same = own[...].astype(f32) + along[...].astype(f32)
    other = beside[...].astype(f32) + across[...].astype(f32)
    rows = jnp.concatenate([same.astype(jnp.bfloat16), other.astype(jnp.bfloat16)], axis=0)
    far_rows = outs[0].shape[0]
    shape = (batch * far_rows, rows.shape[0])
    away, piece, core, slot = split(iota(shape, 0), PIECES, CORES, capacity)
    from_other, from_piece, from_away, from_slot = split(iota(shape, 1), PIECES, batch, capacity)
    match = (away == from_away) & (slot == from_slot) & (piece == from_piece)
    sent = move(match & ((core != core_index()) == (from_other == 1)), rows)
    for d, out in enumerate(outs):
        out[...] = sent[d * far_rows : (d + 1) * far_rows]


def combine_kernel(chips, picks_ref, gains_ref, *refs):
    ins, out = refs[:chips], refs[chips]
    wide = ins[0].shape[1]
    top, toks = gains_ref.shape
    picked = dot(picks_ref[...], below(ins))
    eye = iota((toks, toks), 0) == iota((toks, toks), 1)
    gains = [
        jnp.sum(jnp.where(eye, gains_ref[k : k + 1, :], 0.0), axis=1, keepdims=True)
        for k in range(top)
    ]
    for p in range(PIECES):
        terms = [
            picked[(k * PIECES + p) * toks : (k * PIECES + p + 1) * toks] * gains[k]
            for k in range(top)
        ]
        out[:, p * wide : (p + 1) * wide] = sum(terms[1:], terms[0]).astype(jnp.bfloat16)


def fetch_kernel(start, count, wide, after, weights, got, done, sems):
    del after
    copies = [
        pltpu.make_async_copy(
            weights.at[pl.ds((start + p) * wide, wide)], got.at[pl.ds(p * wide, wide)], sems.at[p]
        )
        for p in range(count)
    ]
    for copy in copies:
        copy.start()
    done[...] = jnp.zeros_like(done)
    for copy in copies:
        copy.wait()


def attend_kernel(chips, capacity, after, lengths, ids_hbm, queries_hbm, cache_hbm, *refs):
    del after
    out_hbm, picks, ids_ref, queries, cache, out, sems = refs
    requests, _, heads = queries.shape
    width = cache.shape[2]
    latent = out.shape[2]
    inward = [pltpu.make_async_copy(ids_hbm, ids_ref, sems.at[0])]
    for r in range(requests):
        inward.append(pltpu.make_async_copy(queries_hbm.at[r], queries.at[r], sems.at[1 + 3 * r]))
        inward.append(pltpu.make_async_copy(cache_hbm.at[r], cache.at[r], sems.at[2 + 3 * r]))
    for copy in inward:
        copy.start()
    inward[0].wait()
    top, toks = ids_ref.shape
    rows = picks.shape[1]
    eye = ones(iota((rows, rows), 0) == iota((rows, rows), 1))
    for k in range(top):
        select = spread_pieces(slot_table(ids_ref[...], chips, capacity, k), chips, capacity)
        picks[k * PIECES * toks : (k + 1) * PIECES * toks] = lax.dot_general(
            select, eye, (((0,), (0,)), ((), ())), preferred_element_type=jnp.float32
        ).astype(jnp.bfloat16)
    outward = []
    for r in range(requests):
        inward[1 + 2 * r].wait()
        inward[2 + 2 * r].wait()
        scores = (
            lax.dot_general(
                queries[r], cache[r], (((0,), (0,)), ((), ())), preferred_element_type=jnp.float32
            )
            * softmax_scale
        )
        scores = jnp.where(iota((heads, width), 1) < lengths[r], scores, -jnp.inf)
        weights = jnp.exp(scores - jnp.max(scores, axis=1, keepdims=True))
        probs = (weights / jnp.sum(weights, axis=1, keepdims=True)).astype(jnp.bfloat16)
        out[r] = lax.dot_general(
            probs,
            cache[r, :latent, :],
            (((1,), (1,)), ((), ())),
            preferred_element_type=jnp.float32,
        ).astype(jnp.bfloat16)
        outward.append(pltpu.make_async_copy(out.at[r], out_hbm.at[r], sems.at[3 + 3 * r]))
        outward[r].start()
    for copy in outward:
        copy.wait()


VMEM = pl.BlockSpec(memory_space=pltpu.VMEM)
HBM = pl.BlockSpec(memory_space=pltpu.HBM)
SMEM = pl.BlockSpec(memory_space=pltpu.SMEM)
DMA = pltpu.SemaphoreType.DMA


def call(kernel, name, out_shape, in_specs, out_specs, scratch, limit, args, flops=0, moved=0):
    return pl.pallas_call(
        kernel,
        name=name,
        out_shape=out_shape,
        in_specs=in_specs,
        out_specs=out_specs,
        scratch_shapes=scratch,
        compiler_params=pltpu.CompilerParams(vmem_limit_bytes=limit),
        cost_estimate=pl.CostEstimate(flops=flops, bytes_accessed=moved, transcendentals=0),
    )(*args)


def paired(n_ep, tokens, expert_ids, gate_weights, w_gate, w_up, w_down, queries, cache, lengths):
    chips = n_ep // CORES
    batches = [(0, 1), (2, 3)]
    batch = 2
    toks, width = tokens.shape
    top = expert_ids.shape[1]
    bf16 = jnp.bfloat16
    capacity = slots_per_expert(toks, top, n_ep)
    wide = width // PIECES
    far = jax.ShapeDtypeStruct((PIECES * CORES * capacity, wide), bf16)
    near = jax.ShapeDtypeStruct((PIECES * batch * capacity, wide), bf16)
    in_hbm = functools.partial(pltpu.with_memory_space_constraint, memory_space=pltpu.HBM)
    got_gate = pltpu.with_memory_space_constraint(w_gate[0], pltpu.VMEM)
    w_up, got_down = in_hbm(w_up[0]), pltpu.with_memory_space_constraint(w_down[0], pltpu.VMEM)
    units = w_up.shape[1]
    ids, gains = in_hbm(expert_ids.T), gate_weights.T

    def to_chip(x, d):
        return lax.ppermute(x, "ep", [(i, i ^ (CORES * d)) for i in range(n_ep)])

    def along(x):
        return lax.ppermute(x, "dp", [(0, 1), (1, 0)])

    def beside(x):
        return lax.ppermute(x, "ep", [(i, i ^ 1) for i in range(n_ep)])

    def across(x):
        return lax.ppermute(x, ("ep", "dp"), [(i, i ^ 3) for i in range(2 * n_ep)])

    packed = call(
        functools.partial(pack_kernel, capacity, chips),
        "pack", (far,) * chips, [HBM] * 2, (VMEM,) * chips,
        [pltpu.VMEM(ids.shape, ids.dtype), pltpu.VMEM(tokens.shape, bf16), DMA((2,))],
        2 * MIB, (ids, in_hbm(tokens)),
    )
    landed = [None] * chips
    landed[0] = packed[0]
    for d in (2, 3, 1):
        landed[d] = to_chip(packed[d], d)
    arrived, got_up = [], []
    begin = 0

    def fetch(count, after):
        nonlocal begin
        fetched, token = call(
            functools.partial(fetch_kernel, begin, count, wide),
            "fetch",
            (pltpu.VMEM((count * wide, units), bf16), jax.ShapeDtypeStruct((8, 128), jnp.float32)),
            [HBM] * 2, (VMEM, VMEM), [DMA((count,))], 1 * MIB, (after, w_up),
            moved=2 * count * wide * units,
        )
        got_up.append(fetched)
        begin += count
        return token

    token = fetch(FETCHED[0], packed[0])
    for chosen, count in zip(batches, FETCHED[1:]):
        same, other = call(
            functools.partial(near_kernel, capacity, batch),
            "near", (near,) * 2, [HBM] + [VMEM] * batch, (VMEM,) * 2, [], 1 * MIB,
            (token, *[landed[d] for d in chosen]),
        )
        core, x, diagonal = beside(other), along(same), across(other)
        arrived += [same, x, core, diagonal]
        token = fetch(count, same)
    n_in = len(arrived)
    rows = n_in * batch * capacity
    parts = call(
        functools.partial(expert_kernel, n_in, len(got_up)),
        "experts", (near,) * n_in, [VMEM] * (n_in + 2 + len(got_up)), (VMEM,) * n_in,
        [
            pltpu.VMEM((PIECES * rows, wide), bf16),
            pltpu.VMEM((rows, units), bf16),
        ],
        4 * MIB, (*arrived, got_gate, *got_up, got_down), flops=6 * rows * width * units,
    )
    back = [None] * chips
    token = parts[0]
    for b in reversed(range(len(batches))):
        own, x, core, diagonal = parts[4 * b : 4 * b + 4]
        if b:
            x, diagonal, core = along(x), across(diagonal), beside(core)
        else:
            core, x, diagonal = beside(core), along(x), across(diagonal)
        sums = call(
            functools.partial(sum_kernel, capacity, batch),
            "sums", (far,) * batch, [HBM] + [VMEM] * 4, (VMEM,) * batch, [], 1 * MIB,
            (token, own, x, core, diagonal),
        )
        token = sums[0]
        for d, value in zip(batches[b], sums):
            back[d] = to_chip(value, d) if d else value
    latent = cache.shape[2] - ROPE
    queries, cache = in_hbm(queries.swapaxes(1, 2)), in_hbm(cache.swapaxes(1, 2))
    requests, _, heads = queries.shape
    attn_out, picks = call(
        functools.partial(attend_kernel, chips, capacity),
        "attend",
        (
            jax.ShapeDtypeStruct((requests, heads, latent), bf16),
            jax.ShapeDtypeStruct((top * PIECES * toks, chips * far.shape[0]), bf16),
        ),
        [HBM, SMEM] + [HBM] * 3, (HBM, VMEM),
        [
            pltpu.VMEM(ids.shape, ids.dtype),
            pltpu.VMEM(queries.shape, bf16),
            pltpu.VMEM(cache.shape, bf16),
            pltpu.VMEM((requests, heads, latent), bf16),
            DMA((1 + 3 * requests,)),
        ],
        6 * MIB, (token, in_hbm(lengths), ids, queries, cache), moved=2 * cache.size,
    )
    moe_out = call(
        functools.partial(combine_kernel, chips),
        "combine", jax.ShapeDtypeStruct(tokens.shape, bf16), [VMEM] * (2 + chips), VMEM, [],
        4 * MIB, (picks, gains, *back),
    )
    return moe_out, attn_out


def solution(mesh):
    placed = (
        P(("group", "ep", "dp"), None),
        P(("group", "ep", "dp"), None),
        P(("group", "ep", "dp"), None),
        P("ep", None, "dp"),
        P("ep", None, "dp"),
        P("ep", "dp", None),
        P(("group", "ep", "dp"), None, None),
        P(("group", "ep", "dp"), None, None),
        P(("group", "ep", "dp")),
    )
    n_ep, n_dp = mesh.shape["ep"], mesh.shape["dp"]
    fits = n_dp == 2 and n_ep == 8
    return jax.shard_map(
        functools.partial(paired, n_ep) if fits else plain,
        mesh=mesh,
        in_specs=placed,
        out_specs=(P(("group", "ep", "dp"), None), P(("group", "ep", "dp"), None, None)),
        check_vma=False,
    )
```

```python
import functools

import jax
import jax.numpy as jnp
from jax import lax
from jax.experimental import pallas as pl
from jax.experimental.pallas import tpu as pltpu
from jax.sharding import PartitionSpec as P

ROPE = 64
CORES = 2
MIB = 1 << 20

softmax_scale = 1.0 / 192.0**0.5


def expert_rows(inputs, w_gate, w_up, w_down):
    gate = jnp.dot(inputs, w_gate[0], preferred_element_type=jnp.float32)
    upper = jnp.dot(inputs, w_up[0], preferred_element_type=jnp.float32)
    hidden = (jax.nn.silu(gate) * upper).astype(jnp.bfloat16)
    return jnp.dot(hidden, w_down[0], preferred_element_type=jnp.float32)


def attend(queries, cache, lengths):
    width = cache.shape[1]
    latent = cache.shape[2] - ROPE
    scores = (
        jnp.einsum("rhc,rlc->rhl", queries, cache, preferred_element_type=jnp.float32)
        * softmax_scale
    )
    valid = jnp.arange(width, dtype=jnp.int32)[None, None, :] < lengths[:, None, None]
    scores = jnp.where(valid, scores, -jnp.inf)
    probs = jax.nn.softmax(scores, axis=-1).astype(jnp.bfloat16)
    return jnp.einsum(
        "rhl,rlc->rhc", probs, cache[:, :, :latent], preferred_element_type=jnp.float32
    ).astype(jnp.bfloat16)


def plain(tokens, expert_ids, gate_weights, w_gate, w_up, w_down, queries, cache, lengths):
    n_ep = lax.axis_size("ep")
    n_dp = lax.axis_size("dp")
    tok_rows = tokens.shape[0]
    width = tokens.shape[1]
    top = expert_ids.shape[1]
    capacity = slots_per_expert(tok_rows, top, n_ep)
    flat_ids = expert_ids.reshape(-1)
    onehot = (flat_ids[:, None] == jnp.arange(n_ep, dtype=jnp.int32)[None, :]).astype(jnp.int32)
    slots = jnp.sum((jnp.cumsum(onehot, axis=0) - 1) * onehot, axis=1)
    target = (flat_ids * capacity + slots).reshape(tok_rows, top)
    places = jnp.arange(n_ep * capacity, dtype=jnp.int32)[:, None, None]
    selector = jnp.sum((places == target[None, :, :]).astype(jnp.bfloat16), axis=2)
    buffer = jnp.dot(selector, tokens, preferred_element_type=jnp.float32).astype(jnp.bfloat16)
    spread = jnp.broadcast_to(
        buffer.reshape(n_ep, 1, capacity, width), (n_ep, n_dp, capacity, width)
    )
    arrived = lax.all_to_all(
        spread.reshape(n_ep * n_dp, capacity, width),
        ("ep", "dp"),
        split_axis=0,
        concat_axis=0,
        tiled=True,
    )
    partial_out = expert_rows(arrived.reshape(-1, width), w_gate, w_up, w_down).astype(jnp.bfloat16)
    returned = lax.all_to_all(
        partial_out.reshape(arrived.shape), ("ep", "dp"), split_axis=0, concat_axis=0, tiled=True
    )
    combined = jnp.sum(returned.reshape(n_ep, n_dp, capacity, width), axis=1, dtype=jnp.float32)
    picked = combined.reshape(n_ep * capacity, width)[target]
    moe_out = jnp.sum(gate_weights[:, :, None] * picked, axis=1).astype(jnp.bfloat16)
    attn_out = attend(queries, cache, lengths)
    return (moe_out, attn_out)


def slots_per_expert(tok_rows, top, n_ep):
    return (3 * tok_rows * top + 2 * n_ep - 1) // (2 * n_ep)


PIECES = 8
FETCHED = (2, 1, 5)


def iota(shape, dim):
    return lax.broadcasted_iota(jnp.int32, shape, dim)


def split(value, *sizes):
    digits = []
    for size in reversed(sizes):
        digits.append(lax.rem(value, size))
        value = lax.div(value, size)
    return [value] + digits[::-1]


def ones(mask):
    return jnp.where(mask, 1.0, 0.0).astype(jnp.bfloat16)


def dot(a, b):
    return jnp.dot(a, b, preferred_element_type=jnp.float32)


def move(mask, rows):
    return dot(ones(mask), rows).astype(jnp.bfloat16)


def below(refs):
    return jnp.concatenate([ref[...] for ref in refs], axis=0)


def chip_index():
    return lax.div(lax.axis_index("ep"), CORES)


def core_index():
    return lax.rem(lax.axis_index("ep"), CORES)


def slot_table(ids, chips, capacity, which=None):
    top, toks = ids.shape
    rows = chips * PIECES * CORES * capacity
    away, piece, core, slot = split(iota((rows, toks), 0), PIECES, CORES, capacity)
    expert = (chip_index() ^ away) * CORES + core
    named = [ids[k : k + 1, :] == expert for k in range(top)]
    any_named = functools.reduce(jnp.logical_or, named)
    before = ones(iota((toks, toks), 0) < iota((toks, toks), 1))
    rank = dot(ones(any_named), before)
    return (any_named if which is None else named[which]) & (rank == slot.astype(jnp.float32))


def spread_pieces(table, chips, capacity):
    rows, toks = table.shape
    repeat = ones(iota((toks, PIECES * toks), 0) == lax.rem(iota((toks, PIECES * toks), 1), toks))
    wide = dot(ones(table), repeat)
    piece = split(iota(wide.shape, 0), PIECES, CORES, capacity)[1]
    return jnp.where(piece == lax.div(iota(wide.shape, 1), toks), wide, 0.0).astype(jnp.bfloat16)


def pack_kernel(capacity, chips, ids_hbm, tok_hbm, *refs):
    outs, (ids_ref, tok_ref, sems) = refs[:chips], refs[chips:]
    copies = [
        pltpu.make_async_copy(ids_hbm, ids_ref, sems.at[0]),
        pltpu.make_async_copy(tok_hbm, tok_ref, sems.at[1]),
    ]
    for copy in copies:
        copy.start()
    copies[0].wait()
    select = spread_pieces(slot_table(ids_ref[...], chips, capacity), chips, capacity)
    copies[1].wait()
    wide = tok_ref.shape[1] // PIECES
    toks = tok_ref[...].astype(jnp.float32)
    stacked = jnp.concatenate(
        [toks[:, k * wide : (k + 1) * wide] for k in range(PIECES)], axis=0
    ).astype(jnp.bfloat16)
    packed = dot(select, stacked).astype(jnp.bfloat16)
    rows = outs[0].shape[0]
    for d, out in enumerate(outs):
        out[...] = packed[d * rows : (d + 1) * rows]


def near_kernel(capacity, batch, after, *refs):
    del after
    ins, (same, other) = refs[:batch], refs[batch:]
    rows = below(ins)
    shape = (same.shape[0], rows.shape[0])
    piece, away, slot = split(iota(shape, 0), batch, capacity)
    from_away, from_piece, from_core, from_slot = split(iota(shape, 1), PIECES, CORES, capacity)
    match = (away == from_away) & (slot == from_slot) & (piece == from_piece)
    same[...] = move(match & (from_core == core_index()), rows)
    other[...] = move(match & (from_core != core_index()), rows)


def expert_kernel(n_in, n_up, *refs):
    ins, gate_ref, ups, refs = refs[:n_in], refs[n_in], refs[n_in + 1 : n_in + 1 + n_up], refs[n_in + 1 + n_up :]
    w_down, outs, (stack, hidden) = refs[0], refs[1 : n_in + 1], refs[n_in + 1 :]
    rows, wide = ins[0].shape
    part = rows // PIECES
    total = n_in * part
    shape = (PIECES * total, n_in * rows)
    piece, who, which = split(iota(shape, 0), n_in, part)
    from_who, from_piece, from_which = split(iota(shape, 1), PIECES, part)
    match = (who == from_who) & (which == from_which) & (piece == from_piece)
    stack[...] = move(match, below(ins))
    blocks = [
        (ref, slice(p * wide, (p + 1) * wide)) for ref in ups for p in range(ref.shape[0] // wide)
    ]
    gate = up = 0.0
    for p in range(PIECES):
        x = stack[p * total : (p + 1) * total]
        gate += dot(x, gate_ref[p * wide : (p + 1) * wide, :])
        ref, span = blocks[p]
        up += dot(x, ref[span, :])
    hidden[...] = (gate / (1.0 + jnp.exp(-gate)) * up).astype(jnp.bfloat16)
    for p in range(PIECES):
        stack[p * total : (p + 1) * total] = dot(
            hidden[...], w_down[:, p * wide : (p + 1) * wide]
        ).astype(jnp.bfloat16)
    shape = (n_in * rows, PIECES * total)
    who, piece, which = split(iota(shape, 0), PIECES, part)
    from_piece, from_who, from_which = split(iota(shape, 1), n_in, part)
    match = (who == from_who) & (which == from_which) & (piece == from_piece)
    back = move(match, stack[...])
    for s, out in enumerate(outs):
        out[...] = back[s * rows : (s + 1) * rows]


def sum_kernel(capacity, batch, after, own, across, along, beside, *outs):
    del after
    f32 = jnp.float32
    same = own[...].astype(f32) + along[...].astype(f32)
    other = beside[...].astype(f32) + across[...].astype(f32)
    rows = jnp.concatenate([same.astype(jnp.bfloat16), other.astype(jnp.bfloat16)], axis=0)
    far_rows = outs[0].shape[0]
    shape = (batch * far_rows, rows.shape[0])
    away, piece, core, slot = split(iota(shape, 0), PIECES, CORES, capacity)
    from_other, from_piece, from_away, from_slot = split(iota(shape, 1), PIECES, batch, capacity)
    match = (away == from_away) & (slot == from_slot) & (piece == from_piece)
    sent = move(match & ((core != core_index()) == (from_other == 1)), rows)
    for d, out in enumerate(outs):
        out[...] = sent[d * far_rows : (d + 1) * far_rows]


def combine_kernel(chips, picks_ref, gains_ref, *refs):
    ins, out = refs[:chips], refs[chips]
    wide = ins[0].shape[1]
    top, toks = gains_ref.shape
    picked = dot(picks_ref[...], below(ins))
    eye = iota((toks, toks), 0) == iota((toks, toks), 1)
    gains = [
        jnp.sum(jnp.where(eye, gains_ref[k : k + 1, :], 0.0), axis=1, keepdims=True)
        for k in range(top)
    ]
    for p in range(PIECES):
        terms = [
            picked[(k * PIECES + p) * toks : (k * PIECES + p + 1) * toks] * gains[k]
            for k in range(top)
        ]
        out[:, p * wide : (p + 1) * wide] = sum(terms[1:], terms[0]).astype(jnp.bfloat16)


def fetch_kernel(start, count, wide, after, weights, got, done, sems):
    del after
    copies = [
        pltpu.make_async_copy(
            weights.at[pl.ds((start + p) * wide, wide)], got.at[pl.ds(p * wide, wide)], sems.at[p]
        )
        for p in range(count)
    ]
    for copy in copies:
        copy.start()
    done[...] = jnp.zeros_like(done)
    for copy in copies:
        copy.wait()


def attend_kernel(chips, capacity, after, lengths, ids_hbm, queries_hbm, cache_hbm, *refs):
    del after
    out_hbm, picks, ids_ref, queries, cache, out, sems = refs
    requests, _, heads = queries.shape
    width = cache.shape[2]
    latent = out.shape[2]
    inward = [pltpu.make_async_copy(ids_hbm, ids_ref, sems.at[0])]
    for r in range(requests):
        inward.append(pltpu.make_async_copy(queries_hbm.at[r], queries.at[r], sems.at[1 + 3 * r]))
        inward.append(pltpu.make_async_copy(cache_hbm.at[r], cache.at[r], sems.at[2 + 3 * r]))
    for copy in inward:
        copy.start()
    inward[0].wait()
    top, toks = ids_ref.shape
    rows = picks.shape[1]
    eye = ones(iota((rows, rows), 0) == iota((rows, rows), 1))
    for k in range(top):
        select = spread_pieces(slot_table(ids_ref[...], chips, capacity, k), chips, capacity)
        picks[k * PIECES * toks : (k + 1) * PIECES * toks] = lax.dot_general(
            select, eye, (((0,), (0,)), ((), ())), preferred_element_type=jnp.float32
        ).astype(jnp.bfloat16)
    outward = []
    for r in range(requests):
        inward[1 + 2 * r].wait()
        inward[2 + 2 * r].wait()
        scores = (
            lax.dot_general(
                queries[r], cache[r], (((0,), (0,)), ((), ())), preferred_element_type=jnp.float32
            )
            * softmax_scale
        )
        scores = jnp.where(iota((heads, width), 1) < lengths[r], scores, -jnp.inf)
        weights = jnp.exp(scores - jnp.max(scores, axis=1, keepdims=True))
        probs = (weights / jnp.sum(weights, axis=1, keepdims=True)).astype(jnp.bfloat16)
        out[r] = lax.dot_general(
            probs,
            cache[r, :latent, :],
            (((1,), (1,)), ((), ())),
            preferred_element_type=jnp.float32,
        ).astype(jnp.bfloat16)
        outward.append(pltpu.make_async_copy(out.at[r], out_hbm.at[r], sems.at[3 + 3 * r]))
        outward[r].start()
    for copy in outward:
        copy.wait()


VMEM = pl.BlockSpec(memory_space=pltpu.VMEM)
HBM = pl.BlockSpec(memory_space=pltpu.HBM)
SMEM = pl.BlockSpec(memory_space=pltpu.SMEM)
DMA = pltpu.SemaphoreType.DMA


def call(kernel, name, out_shape, in_specs, out_specs, scratch, limit, args, flops=0, moved=0):
    return pl.pallas_call(
        kernel,
        name=name,
        out_shape=out_shape,
        in_specs=in_specs,
        out_specs=out_specs,
        scratch_shapes=scratch,
        compiler_params=pltpu.CompilerParams(vmem_limit_bytes=limit),
        cost_estimate=pl.CostEstimate(flops=flops, bytes_accessed=moved, transcendentals=0),
    )(*args)


def paired(n_ep, tokens, expert_ids, gate_weights, w_gate, w_up, w_down, queries, cache, lengths):
    chips = n_ep // CORES
    batches = [(0, 1), (2, 3)]
    batch = 2
    toks, width = tokens.shape
    top = expert_ids.shape[1]
    bf16 = jnp.bfloat16
    capacity = slots_per_expert(toks, top, n_ep)
    wide = width // PIECES
    far = jax.ShapeDtypeStruct((PIECES * CORES * capacity, wide), bf16)
    near = jax.ShapeDtypeStruct((PIECES * batch * capacity, wide), bf16)
    in_hbm = functools.partial(pltpu.with_memory_space_constraint, memory_space=pltpu.HBM)
    got_gate = pltpu.with_memory_space_constraint(w_gate[0], pltpu.VMEM)
    w_up, got_down = in_hbm(w_up[0]), pltpu.with_memory_space_constraint(w_down[0], pltpu.VMEM)
    units = w_up.shape[1]
    ids, gains = in_hbm(expert_ids.T), gate_weights.T

    def to_chip(x, d):
        return lax.ppermute(x, "ep", [(i, i ^ (CORES * d)) for i in range(n_ep)])

    def along(x):
        return lax.ppermute(x, "dp", [(0, 1), (1, 0)])

    def beside(x):
        return lax.ppermute(x, "ep", [(i, i ^ 1) for i in range(n_ep)])

    def across(x):
        return lax.ppermute(x, ("ep", "dp"), [(i, i ^ 3) for i in range(2 * n_ep)])

    packed = call(
        functools.partial(pack_kernel, capacity, chips),
        "pack", (far,) * chips, [HBM] * 2, (VMEM,) * chips,
        [pltpu.VMEM(ids.shape, ids.dtype), pltpu.VMEM(tokens.shape, bf16), DMA((2,))],
        2 * MIB, (ids, in_hbm(tokens)),
    )
    landed = [None] * chips
    landed[0] = packed[0]
    for d in (2, 3, 1):
        landed[d] = to_chip(packed[d], d)
    arrived, got_up = [], []
    begin = 0

    def fetch(count, after):
        nonlocal begin
        fetched, token = call(
            functools.partial(fetch_kernel, begin, count, wide),
            "fetch",
            (pltpu.VMEM((count * wide, units), bf16), jax.ShapeDtypeStruct((8, 128), jnp.float32)),
            [HBM] * 2, (VMEM, VMEM), [DMA((count,))], 1 * MIB, (after, w_up),
            moved=2 * count * wide * units,
        )
        got_up.append(fetched)
        begin += count
        return token

    token = fetch(FETCHED[0], packed[0])
    for chosen, count in zip(batches, FETCHED[1:]):
        same, other = call(
            functools.partial(near_kernel, capacity, batch),
            "near", (near,) * 2, [HBM] + [VMEM] * batch, (VMEM,) * 2, [], 1 * MIB,
            (token, *[landed[d] for d in chosen]),
        )
        core, x, diagonal = beside(other), along(same), across(other)
        arrived += [same, x, core, diagonal]
        token = fetch(count, same)
    n_in = len(arrived)
    rows = n_in * batch * capacity
    parts = call(
        functools.partial(expert_kernel, n_in, len(got_up)),
        "experts", (near,) * n_in, [VMEM] * (n_in + 2 + len(got_up)), (VMEM,) * n_in,
        [
            pltpu.VMEM((PIECES * rows, wide), bf16),
            pltpu.VMEM((rows, units), bf16),
        ],
        4 * MIB, (*arrived, got_gate, *got_up, got_down), flops=6 * rows * width * units,
    )
    back = [None] * chips
    token = parts[0]
    for b in reversed(range(len(batches))):
        own, x, core, diagonal = parts[4 * b : 4 * b + 4]
        if b:
            x, diagonal, core = along(x), across(diagonal), beside(core)
        else:
            core, x, diagonal = beside(core), along(x), across(diagonal)
        sums = call(
            functools.partial(sum_kernel, capacity, batch),
            "sums", (far,) * batch, [HBM] + [VMEM] * 4, (VMEM,) * batch, [], 1 * MIB,
            (token, own, diagonal, x, core),
        )
        token = sums[0]
        for d, value in zip(batches[b], sums):
            back[d] = to_chip(value, d) if d else value
    latent = cache.shape[2] - ROPE
    queries, cache = in_hbm(queries.swapaxes(1, 2)), in_hbm(cache.swapaxes(1, 2))
    requests, _, heads = queries.shape
    attn_out, picks = call(
        functools.partial(attend_kernel, chips, capacity),
        "attend",
        (
            jax.ShapeDtypeStruct((requests, heads, latent), bf16),
            jax.ShapeDtypeStruct((top * PIECES * toks, chips * far.shape[0]), bf16),
        ),
        [HBM, SMEM] + [HBM] * 3, (HBM, VMEM),
        [
            pltpu.VMEM(ids.shape, ids.dtype),
            pltpu.VMEM(queries.shape, bf16),
            pltpu.VMEM(cache.shape, bf16),
            pltpu.VMEM((requests, heads, latent), bf16),
            DMA((1 + 3 * requests,)),
        ],
        6 * MIB, (token, in_hbm(lengths), ids, queries, cache), moved=2 * cache.size,
    )
    moe_out = call(
        functools.partial(combine_kernel, chips),
        "combine", jax.ShapeDtypeStruct(tokens.shape, bf16), [VMEM] * (2 + chips), VMEM, [],
        4 * MIB, (picks, gains, *back),
    )
    return moe_out, attn_out


def solution(mesh):
    placed = (
        P(("group", "ep", "dp"), None),
        P(("group", "ep", "dp"), None),
        P(("group", "ep", "dp"), None),
        P("ep", None, "dp"),
        P("ep", None, "dp"),
        P("ep", "dp", None),
        P(("group", "ep", "dp"), None, None),
        P(("group", "ep", "dp"), None, None),
        P(("group", "ep", "dp")),
    )
    n_ep, n_dp = mesh.shape["ep"], mesh.shape["dp"]
    fits = n_dp == 2 and n_ep == 8
    return jax.shard_map(
        functools.partial(paired, n_ep) if fits else plain,
        mesh=mesh,
        in_specs=placed,
        out_specs=(P(("group", "ep", "dp"), None), P(("group", "ep", "dp"), None, None)),
        check_vma=False,
    )
```

```python
import functools

import jax
import jax.numpy as jnp
from jax import lax
from jax.experimental import pallas as pl
from jax.experimental.pallas import tpu as pltpu
from jax.sharding import PartitionSpec as P

ROPE = 64
CORES = 2
MIB = 1 << 20

softmax_scale = 1.0 / 192.0**0.5


def expert_rows(inputs, w_gate, w_up, w_down):
    gate = jnp.dot(inputs, w_gate[0], preferred_element_type=jnp.float32)
    upper = jnp.dot(inputs, w_up[0], preferred_element_type=jnp.float32)
    hidden = (jax.nn.silu(gate) * upper).astype(jnp.bfloat16)
    return jnp.dot(hidden, w_down[0], preferred_element_type=jnp.float32)


def attend(queries, cache, lengths):
    width = cache.shape[1]
    latent = cache.shape[2] - ROPE
    scores = (
        jnp.einsum("rhc,rlc->rhl", queries, cache, preferred_element_type=jnp.float32)
        * softmax_scale
    )
    valid = jnp.arange(width, dtype=jnp.int32)[None, None, :] < lengths[:, None, None]
    scores = jnp.where(valid, scores, -jnp.inf)
    probs = jax.nn.softmax(scores, axis=-1).astype(jnp.bfloat16)
    return jnp.einsum(
        "rhl,rlc->rhc", probs, cache[:, :, :latent], preferred_element_type=jnp.float32
    ).astype(jnp.bfloat16)


def plain(tokens, expert_ids, gate_weights, w_gate, w_up, w_down, queries, cache, lengths):
    n_ep = lax.axis_size("ep")
    n_dp = lax.axis_size("dp")
    tok_rows = tokens.shape[0]
    width = tokens.shape[1]
    top = expert_ids.shape[1]
    capacity = slots_per_expert(tok_rows, top, n_ep)
    flat_ids = expert_ids.reshape(-1)
    onehot = (flat_ids[:, None] == jnp.arange(n_ep, dtype=jnp.int32)[None, :]).astype(jnp.int32)
    slots = jnp.sum((jnp.cumsum(onehot, axis=0) - 1) * onehot, axis=1)
    target = (flat_ids * capacity + slots).reshape(tok_rows, top)
    places = jnp.arange(n_ep * capacity, dtype=jnp.int32)[:, None, None]
    selector = jnp.sum((places == target[None, :, :]).astype(jnp.bfloat16), axis=2)
    buffer = jnp.dot(selector, tokens, preferred_element_type=jnp.float32).astype(jnp.bfloat16)
    spread = jnp.broadcast_to(
        buffer.reshape(n_ep, 1, capacity, width), (n_ep, n_dp, capacity, width)
    )
    arrived = lax.all_to_all(
        spread.reshape(n_ep * n_dp, capacity, width),
        ("ep", "dp"),
        split_axis=0,
        concat_axis=0,
        tiled=True,
    )
    partial_out = expert_rows(arrived.reshape(-1, width), w_gate, w_up, w_down).astype(jnp.bfloat16)
    returned = lax.all_to_all(
        partial_out.reshape(arrived.shape), ("ep", "dp"), split_axis=0, concat_axis=0, tiled=True
    )
    combined = jnp.sum(returned.reshape(n_ep, n_dp, capacity, width), axis=1, dtype=jnp.float32)
    picked = combined.reshape(n_ep * capacity, width)[target]
    moe_out = jnp.sum(gate_weights[:, :, None] * picked, axis=1).astype(jnp.bfloat16)
    attn_out = attend(queries, cache, lengths)
    return (moe_out, attn_out)


def slots_per_expert(tok_rows, top, n_ep):
    return (3 * tok_rows * top + 2 * n_ep - 1) // (2 * n_ep)


PIECES = 8
CUTS = 4
FETCHED = (1, 1, 6)


def iota(shape, dim):
    return lax.broadcasted_iota(jnp.int32, shape, dim)


def split(value, *sizes):
    digits = []
    for size in reversed(sizes):
        digits.append(lax.rem(value, size))
        value = lax.div(value, size)
    return [value] + digits[::-1]


def ones(mask):
    return jnp.where(mask, 1.0, 0.0).astype(jnp.bfloat16)


def dot(a, b):
    return jnp.dot(a, b, preferred_element_type=jnp.float32)


def move(mask, rows):
    return dot(ones(mask), rows).astype(jnp.bfloat16)


def below(refs):
    return jnp.concatenate([ref[...] for ref in refs], axis=0)


def chip_index():
    return lax.div(lax.axis_index("ep"), CORES)


def core_index():
    return lax.rem(lax.axis_index("ep"), CORES)


def slot_table(ids, chips, capacity, which=None):
    top, toks = ids.shape
    rows = chips * PIECES * CORES * capacity
    away, piece, core, slot = split(iota((rows, toks), 0), PIECES, CORES, capacity)
    expert = (chip_index() ^ away) * CORES + core
    named = [ids[k : k + 1, :] == expert for k in range(top)]
    any_named = functools.reduce(jnp.logical_or, named)
    before = ones(iota((toks, toks), 0) < iota((toks, toks), 1))
    rank = dot(ones(any_named), before)
    return (any_named if which is None else named[which]) & (rank == slot.astype(jnp.float32))


def spread_pieces(table, chips, capacity):
    rows, toks = table.shape
    repeat = ones(iota((toks, PIECES * toks), 0) == lax.rem(iota((toks, PIECES * toks), 1), toks))
    wide = dot(ones(table), repeat)
    piece = split(iota(wide.shape, 0), PIECES, CORES, capacity)[1]
    return jnp.where(piece == lax.div(iota(wide.shape, 1), toks), wide, 0.0).astype(jnp.bfloat16)


def pack_kernel(capacity, chips, ids_hbm, tok_hbm, *refs):
    outs, (ids_ref, tok_ref, sems) = refs[:chips], refs[chips:]
    copies = [
        pltpu.make_async_copy(ids_hbm, ids_ref, sems.at[0]),
        pltpu.make_async_copy(tok_hbm, tok_ref, sems.at[1]),
    ]
    for copy in copies:
        copy.start()
    copies[0].wait()
    select = spread_pieces(slot_table(ids_ref[...], chips, capacity), chips, capacity)
    copies[1].wait()
    wide = tok_ref.shape[1] // PIECES
    toks = tok_ref[...].astype(jnp.float32)
    stacked = jnp.concatenate(
        [toks[:, k * wide : (k + 1) * wide] for k in range(PIECES)], axis=0
    ).astype(jnp.bfloat16)
    packed = dot(select, stacked).astype(jnp.bfloat16)
    rows = outs[0].shape[0]
    for d, out in enumerate(outs):
        out[...] = packed[d * rows : (d + 1) * rows]


def near_kernel(capacity, batch, after, *refs):
    del after
    ins, (same, other) = refs[:batch], refs[batch:]
    rows = below(ins)
    shape = (same.shape[0], rows.shape[0])
    piece, away, slot = split(iota(shape, 0), batch, capacity)
    from_away, from_piece, from_core, from_slot = split(iota(shape, 1), PIECES, CORES, capacity)
    match = (away == from_away) & (slot == from_slot) & (piece == from_piece)
    same[...] = move(match & (from_core == core_index()), rows)
    other[...] = move(match & (from_core != core_index()), rows)


def expert_kernel(n_in, n_up, *refs):
    ins, gate_ref, ups, refs = refs[:n_in], refs[n_in], refs[n_in + 1 : n_in + 1 + n_up], refs[n_in + 1 + n_up :]
    w_down, outs, (stack, hidden) = refs[0], refs[1 : n_in + 1], refs[n_in + 1 :]
    rows, wide = ins[0].shape
    part = rows // PIECES
    total = n_in * part
    shape = (PIECES * total, n_in * rows)
    piece, who, which = split(iota(shape, 0), n_in, part)
    from_who, from_piece, from_which = split(iota(shape, 1), PIECES, part)
    match = (who == from_who) & (which == from_which) & (piece == from_piece)
    stack[...] = move(match, below(ins))
    blocks = [
        (ref, slice(p * wide, (p + 1) * wide)) for ref in ups for p in range(ref.shape[0] // wide)
    ]
    gate = up = 0.0
    for p in range(PIECES):
        x = stack[p * total : (p + 1) * total]
        gate += dot(x, gate_ref[p * wide : (p + 1) * wide, :])
        ref, span = blocks[p]
        up += dot(x, ref[span, :])
    hidden[...] = (gate / (1.0 + jnp.exp(-gate)) * up).astype(jnp.bfloat16)
    for p in range(PIECES):
        stack[p * total : (p + 1) * total] = dot(
            hidden[...], w_down[:, p * wide : (p + 1) * wide]
        ).astype(jnp.bfloat16)
    shape = (n_in * rows, PIECES * total)
    who, piece, which = split(iota(shape, 0), PIECES, part)
    from_piece, from_who, from_which = split(iota(shape, 1), n_in, part)
    match = (who == from_who) & (which == from_which) & (piece == from_piece)
    back = move(match, stack[...])
    for s, out in enumerate(outs):
        out[...] = back[s * rows : (s + 1) * rows]


def sum_kernel(capacity, batch, after, own, across, along, beside, *outs):
    del after
    f32 = jnp.float32
    same = own[...].astype(f32) + along[...].astype(f32)
    other = beside[...].astype(f32) + across[...].astype(f32)
    rows = jnp.concatenate([same.astype(jnp.bfloat16), other.astype(jnp.bfloat16)], axis=0)
    far_rows = outs[0].shape[0]
    shape = (batch * far_rows, rows.shape[0])
    away, piece, core, slot = split(iota(shape, 0), PIECES, CORES, capacity)
    from_other, from_piece, from_away, from_slot = split(iota(shape, 1), PIECES, batch, capacity)
    match = (away == from_away) & (slot == from_slot) & (piece == from_piece)
    sent = move(match & ((core != core_index()) == (from_other == 1)), rows)
    for d, out in enumerate(outs):
        out[...] = sent[d * far_rows : (d + 1) * far_rows]


def combine_kernel(chips, picks_ref, gains_ref, *refs):
    ins, out = refs[:chips], refs[chips]
    wide = ins[0].shape[1]
    top, toks = gains_ref.shape
    picked = dot(picks_ref[...], below(ins))
    eye = iota((toks, toks), 0) == iota((toks, toks), 1)
    gains = [
        jnp.sum(jnp.where(eye, gains_ref[k : k + 1, :], 0.0), axis=1, keepdims=True)
        for k in range(top)
    ]
    for p in range(PIECES):
        terms = [
            picked[(k * PIECES + p) * toks : (k * PIECES + p + 1) * toks] * gains[k]
            for k in range(top)
        ]
        out[:, p * wide : (p + 1) * wide] = sum(terms[1:], terms[0]).astype(jnp.bfloat16)


def fetch_kernel(start, count, wide, after, weights, got, done, sems):
    del after
    rows = wide // CUTS
    copies = [
        pltpu.make_async_copy(
            weights.at[pl.ds(start * wide + p * rows, rows)],
            got.at[pl.ds(p * rows, rows)],
            sems.at[p],
        )
        for p in range(count * CUTS)
    ]
    for copy in copies:
        copy.start()
    done[...] = jnp.zeros_like(done)
    for copy in copies:
        copy.wait()


def attend_kernel(chips, capacity, after, lengths, ids_hbm, queries_hbm, cache_hbm, *refs):
    del after
    out_hbm, picks, ids_ref, queries, cache, out, sems = refs
    requests, _, heads = queries.shape
    width = cache.shape[2]
    latent = out.shape[2]
    inward = [pltpu.make_async_copy(ids_hbm, ids_ref, sems.at[0])]
    for r in range(requests):
        inward.append(pltpu.make_async_copy(queries_hbm.at[r], queries.at[r], sems.at[1 + 3 * r]))
        inward.append(pltpu.make_async_copy(cache_hbm.at[r], cache.at[r], sems.at[2 + 3 * r]))
    for copy in inward:
        copy.start()
    inward[0].wait()
    top, toks = ids_ref.shape
    rows = picks.shape[1]
    eye = ones(iota((rows, rows), 0) == iota((rows, rows), 1))
    for k in range(top):
        select = spread_pieces(slot_table(ids_ref[...], chips, capacity, k), chips, capacity)
        picks[k * PIECES * toks : (k + 1) * PIECES * toks] = lax.dot_general(
            select, eye, (((0,), (0,)), ((), ())), preferred_element_type=jnp.float32
        ).astype(jnp.bfloat16)
    outward = []
    for r in range(requests):
        inward[1 + 2 * r].wait()
        inward[2 + 2 * r].wait()
        scores = (
            lax.dot_general(
                queries[r], cache[r], (((0,), (0,)), ((), ())), preferred_element_type=jnp.float32
            )
            * softmax_scale
        )
        scores = jnp.where(iota((heads, width), 1) < lengths[r], scores, -jnp.inf)
        weights = jnp.exp(scores - jnp.max(scores, axis=1, keepdims=True))
        probs = (weights / jnp.sum(weights, axis=1, keepdims=True)).astype(jnp.bfloat16)
        out[r] = lax.dot_general(
            probs,
            cache[r, :latent, :],
            (((1,), (1,)), ((), ())),
            preferred_element_type=jnp.float32,
        ).astype(jnp.bfloat16)
        outward.append(pltpu.make_async_copy(out.at[r], out_hbm.at[r], sems.at[3 + 3 * r]))
        outward[r].start()
    for copy in outward:
        copy.wait()


VMEM = pl.BlockSpec(memory_space=pltpu.VMEM)
HBM = pl.BlockSpec(memory_space=pltpu.HBM)
SMEM = pl.BlockSpec(memory_space=pltpu.SMEM)
DMA = pltpu.SemaphoreType.DMA


def call(kernel, name, out_shape, in_specs, out_specs, scratch, limit, args, flops=0, moved=0):
    return pl.pallas_call(
        kernel,
        name=name,
        out_shape=out_shape,
        in_specs=in_specs,
        out_specs=out_specs,
        scratch_shapes=scratch,
        compiler_params=pltpu.CompilerParams(vmem_limit_bytes=limit),
        cost_estimate=pl.CostEstimate(flops=flops, bytes_accessed=moved, transcendentals=0),
    )(*args)


def paired(n_ep, tokens, expert_ids, gate_weights, w_gate, w_up, w_down, queries, cache, lengths):
    chips = n_ep // CORES
    batches = [(0, 1), (2, 3)]
    batch = 2
    toks, width = tokens.shape
    top = expert_ids.shape[1]
    bf16 = jnp.bfloat16
    capacity = slots_per_expert(toks, top, n_ep)
    wide = width // PIECES
    far = jax.ShapeDtypeStruct((PIECES * CORES * capacity, wide), bf16)
    near = jax.ShapeDtypeStruct((PIECES * batch * capacity, wide), bf16)
    in_hbm = functools.partial(pltpu.with_memory_space_constraint, memory_space=pltpu.HBM)
    got_gate = pltpu.with_memory_space_constraint(w_gate[0], pltpu.VMEM)
    w_up, got_down = in_hbm(w_up[0]), pltpu.with_memory_space_constraint(w_down[0], pltpu.VMEM)
    units = w_up.shape[1]
    ids, gains = in_hbm(expert_ids.T), gate_weights.T

    def to_chip(x, d):
        return lax.ppermute(x, "ep", [(i, i ^ (CORES * d)) for i in range(n_ep)])

    def along(x):
        return lax.ppermute(x, "dp", [(0, 1), (1, 0)])

    def beside(x):
        return lax.ppermute(x, "ep", [(i, i ^ 1) for i in range(n_ep)])

    def across(x):
        return lax.ppermute(x, ("ep", "dp"), [(i, i ^ 3) for i in range(2 * n_ep)])

    packed = call(
        functools.partial(pack_kernel, capacity, chips),
        "pack", (far,) * chips, [HBM] * 2, (VMEM,) * chips,
        [pltpu.VMEM(ids.shape, ids.dtype), pltpu.VMEM(tokens.shape, bf16), DMA((2,))],
        2 * MIB, (ids, in_hbm(tokens)),
    )
    landed = [None] * chips
    landed[0] = packed[0]
    for d in (2, 3, 1):
        landed[d] = to_chip(packed[d], d)
    arrived, got_up = [], []
    begin = 0

    def fetch(count, after):
        nonlocal begin
        fetched, token = call(
            functools.partial(fetch_kernel, begin, count, wide),
            "fetch",
            (pltpu.VMEM((count * wide, units), bf16), jax.ShapeDtypeStruct((8, 128), jnp.float32)),
            [HBM] * 2, (VMEM, VMEM), [DMA((count * CUTS,))], 1 * MIB, (after, w_up),
            moved=2 * count * wide * units,
        )
        got_up.append(fetched)
        begin += count
        return token

    token = fetch(FETCHED[0], packed[0])
    for chosen, count in zip(batches, FETCHED[1:]):
        same, other = call(
            functools.partial(near_kernel, capacity, batch),
            "near", (near,) * 2, [HBM] + [VMEM] * batch, (VMEM,) * 2, [], 1 * MIB,
            (token, *[landed[d] for d in chosen]),
        )
        core, x, diagonal = beside(other), along(same), across(other)
        arrived += [same, x, core, diagonal]
        token = fetch(count, same)
    n_in = len(arrived)
    rows = n_in * batch * capacity
    parts = call(
        functools.partial(expert_kernel, n_in, len(got_up)),
        "experts", (near,) * n_in, [VMEM] * (n_in + 2 + len(got_up)), (VMEM,) * n_in,
        [
            pltpu.VMEM((PIECES * rows, wide), bf16),
            pltpu.VMEM((rows, units), bf16),
        ],
        4 * MIB, (*arrived, got_gate, *got_up, got_down), flops=6 * rows * width * units,
    )
    back = [None] * chips
    token = parts[0]
    for b in reversed(range(len(batches))):
        own, x, core, diagonal = parts[4 * b : 4 * b + 4]
        if b:
            x, diagonal, core = along(x), across(diagonal), beside(core)
        else:
            core, x, diagonal = beside(core), along(x), across(diagonal)
        sums = call(
            functools.partial(sum_kernel, capacity, batch),
            "sums", (far,) * batch, [HBM] + [VMEM] * 4, (VMEM,) * batch, [], 1 * MIB,
            (token, own, diagonal, x, core),
        )
        token = sums[0]
        for d, value in zip(batches[b], sums):
            back[d] = to_chip(value, d) if d else value
    latent = cache.shape[2] - ROPE
    queries, cache = in_hbm(queries.swapaxes(1, 2)), in_hbm(cache.swapaxes(1, 2))
    requests, _, heads = queries.shape
    attn_out, picks = call(
        functools.partial(attend_kernel, chips, capacity),
        "attend",
        (
            jax.ShapeDtypeStruct((requests, heads, latent), bf16),
            jax.ShapeDtypeStruct((top * PIECES * toks, chips * far.shape[0]), bf16),
        ),
        [HBM, SMEM] + [HBM] * 3, (HBM, VMEM),
        [
            pltpu.VMEM(ids.shape, ids.dtype),
            pltpu.VMEM(queries.shape, bf16),
            pltpu.VMEM(cache.shape, bf16),
            pltpu.VMEM((requests, heads, latent), bf16),
            DMA((1 + 3 * requests,)),
        ],
        6 * MIB, (token, in_hbm(lengths), ids, queries, cache), moved=2 * cache.size,
    )
    moe_out = call(
        functools.partial(combine_kernel, chips),
        "combine", jax.ShapeDtypeStruct(tokens.shape, bf16), [VMEM] * (2 + chips), VMEM, [],
        4 * MIB, (picks, gains, *back),
    )
    return moe_out, attn_out


def solution(mesh):
    placed = (
        P(("group", "ep", "dp"), None),
        P(("group", "ep", "dp"), None),
        P(("group", "ep", "dp"), None),
        P("ep", None, "dp"),
        P("ep", None, "dp"),
        P("ep", "dp", None),
        P(("group", "ep", "dp"), None, None),
        P(("group", "ep", "dp"), None, None),
        P(("group", "ep", "dp")),
    )
    n_ep, n_dp = mesh.shape["ep"], mesh.shape["dp"]
    fits = n_dp == 2 and n_ep == 8
    return jax.shard_map(
        functools.partial(paired, n_ep) if fits else plain,
        mesh=mesh,
        in_specs=placed,
        out_specs=(P(("group", "ep", "dp"), None), P(("group", "ep", "dp"), None, None)),
        check_vma=False,
    )
```
